32 devices in a mesh: section: 4 (over y, x), tensor: 8 (over z, core).
Axes of the slice: x: 2, y: 2, z: 4, core: 2. Of those that a mesh axis runs over, the one named last changes fastest.
Arguments:
- x_in: bfloat16 [4, 512, 4096], P('section', 'tensor'), may hold values from -40 to 40
- grad_out: bfloat16 [4, 512, 4096], P('section', 'tensor'), may hold values from -50 to 50
- gain: float32 [4, 4096], P('section'), may hold values from 0.5 to 1.5
- w_val: bfloat16 [4, 4096, 4096], P('section', 'tensor'), may hold values from -0.09375 to 0.09375
- w_out: bfloat16 [4, 4096, 4096], P('section', 'tensor'), may hold values from -0.09375 to 0.09375
- filt: float32 [4, 3, 4096], P('section', None, 'tensor'), may hold values from -3 to 3
- tail: bfloat16 [4, 2, 4096], P('section', None, 'tensor'), may hold values from -6 to 6
- micro_index: int32 [4], P('section'), may hold values from 0 to 15
Outputs:
- grad_in: bfloat16 [4, 512, 4096], P('section', 'tensor')
- grad_w_val: bfloat16 [4, 4096, 4096], P('section', 'tensor')
- grad_w_out: bfloat16 [4, 4096, 4096], P('section', 'tensor')
- grad_filter: float32 [4, 3, 4096], P('section', None, 'tensor')
- grad_tail: float32 [4, 2, 4096], P('section', None, 'tensor')
- grad_gain: float32 [4, 4096], P('section')
The draws below stay inside these ranges and needn't reach their ends.
All inputs are finite; a program needn't handle non-finite values.
Results may differ from the reference program's by a relative error of at most 0.023.
Values may be sent and summed in bfloat16 or wider, within the bound.
A program may use at most 64 MiB of HBM per device.

```python
import math
import jax
import jax.numpy as jnp
from jax import lax

D = 4096
C = 4096
TAPS = 3
MICROS = 16
SLICE = 512
SECTIONS = 4
N_TENSOR = 8


def draw_x_in(key, part):
    key_base, key_rows, key_cols = jax.random.split(jax.random.fold_in(key, 11), 3)
    shape = (SECTIONS, SLICE, D)
    row_scale = jnp.exp(jax.random.uniform(key_rows, (SECTIONS, SLICE, 1), jnp.float32, math.log(0.3), math.log(3.0)))
    col_scale = jnp.exp(jax.random.uniform(key_cols, (SECTIONS, 1, D), jnp.float32, math.log(0.3), math.log(3.0)))
    base = jnp.clip(jax.random.normal(key_base, shape, jnp.float32), -4.0, 4.0)
    return (base * row_scale * col_scale).astype(jnp.bfloat16)


def draw_grad_out(key, part):
    key_base, key_rows = jax.random.split(jax.random.fold_in(key, 23), 2)
    shape = (SECTIONS, SLICE, D)
    position = jnp.arange(SLICE, dtype=jnp.float32) / max(SLICE - 1, 1)
    jitter = jnp.exp(jax.random.uniform(key_rows, (SECTIONS, SLICE, 1), jnp.float32, math.log(0.7), math.log(1.4)))
    rising = 1.0 + 2.0 * position
    base = jnp.clip(jax.random.normal(key_base, shape, jnp.float32), -4.0, 4.0)
    return (base * rising[None, :, None] * jitter).astype(jnp.bfloat16)


def with_ends(entries, stream_key, low, largest):
    longest = entries.shape.index(max(entries.shape))
    spots = []
    for shift in (0, 1):
        where = [jax.random.randint(jax.random.fold_in(stream_key, axis), (), 0, length) for axis, length in enumerate(entries.shape)]
        where[longest] = (where[longest] + shift) % entries.shape[longest]
        spots.append(tuple(where))
    return entries.at[spots[0]].set(low).at[spots[1]].set(largest)


def block_levels(rng, extent, cuts, least, largest):
    level = 1.0
    for axis_at, shards_of in cuts:
        steps = jax.random.uniform(jax.random.fold_in(jax.random.fold_in(rng, 6), axis_at), (shards_of,), jnp.float32, least / len(cuts), largest / len(cuts))
        level = level * jnp.repeat(jnp.exp(steps), extent[axis_at] // shards_of).reshape((-1,) + (1,) * (len(extent) - 1 - axis_at))
    return level


def scatter_about(own_key, dims, width, limit, pieces=(), kind=jnp.bfloat16):
    entries = jax.random.normal(own_key, dims, jnp.float32) * width
    if len(pieces) > 0:
        entries = block_levels(own_key, dims, pieces, -0.22, 0.18) * entries
    return jnp.clip(entries, min=-limit, max=limit).astype(kind)


def setup_inputs(seed: int = 0) -> dict:
    key_list = jax.random.split(jax.random.key(seed), 9)
    x_in = draw_x_in(jax.random.fold_in(key_list[8], 71), 0)
    grad_out = draw_grad_out(jax.random.fold_in(key_list[8], 71), 0)
    gain = jnp.clip(1.0 + 0.1 * jax.random.normal(key_list[2], (SECTIONS, D), jnp.float32), 0.5, 1.5)
    w_val = scatter_about(key_list[3], (SECTIONS, C, D), D ** -0.5, 0.09375, ((0, 4), (1, 8)))
    w_out = scatter_about(key_list[4], (SECTIONS, C, D), C ** -0.5, 0.09375, ((0, 4), (1, 8)))
    filt = scatter_about(key_list[5], (SECTIONS, TAPS, C), 0.5, 3.0, ((0, 4), (2, 8)), jnp.float32)
    tail = scatter_about(key_list[6], (SECTIONS, TAPS - 1, C), 1.0, 6.0, ((0, 4), (2, 8)))
    micro_index = with_ends(jax.random.randint(key_list[7], (SECTIONS,), 0, MICROS), jax.random.fold_in(key_list[7], 1), 0, MICROS - 1).astype(jnp.int32)
    return dict(x_in=x_in, grad_out=grad_out, gain=gain, w_val=w_val, w_out=w_out, filt=filt, tail=tail, micro_index=micro_index)


EPSILON = 1e-06

def section_backward(x_in, grad_out, gain, w_val, w_out, filt, tail, micro_now):
    seq_len = x_in.shape[0]
    local_ch = C // N_TENSOR
    x_float = x_in.astype(jnp.float32)
    inv_rms = lax.rsqrt(lax.optimization_barrier(jnp.mean(x_float * x_float, axis=-1, keepdims=True)) + EPSILON)
    normed = (x_float * inv_rms * gain).astype(jnp.bfloat16)
    values = jnp.dot(normed, w_val.T, preferred_element_type=jnp.float32).astype(jnp.bfloat16)
    has_tail = micro_now > 0
    lead_rows = jnp.where(has_tail, tail, jnp.zeros_like(tail))
    extended = jnp.concatenate([lead_rows, values], axis=0).astype(jnp.float32)
    conv_out = filt[0] * extended[TAPS - 1:TAPS - 1 + seq_len]
    for tap in range(1, TAPS):
        conv_out = conv_out + filt[tap] * extended[TAPS - 1 - tap:TAPS - 1 - tap + seq_len]
    gate_sig = jax.nn.sigmoid(conv_out)
    gated = (conv_out * gate_sig).astype(jnp.bfloat16)
    grad_gated = jnp.dot(grad_out, w_out.T, preferred_element_type=jnp.float32)
    grad_conv = grad_gated * gate_sig * (1.0 + conv_out * (1.0 - gate_sig))
    grad_filter = jnp.stack([lax.optimization_barrier(jnp.sum(grad_conv * extended[TAPS - 1 - tap:TAPS - 1 - tap + seq_len], axis=0)) for tap in range(TAPS)])
    padded = jnp.pad(grad_conv, ((TAPS - 1, TAPS - 1), (0, 0)))
    grad_ext = filt[0] * padded[0:seq_len + TAPS - 1]
    for tap in range(1, TAPS):
        grad_ext = grad_ext + filt[tap] * padded[tap:tap + seq_len + TAPS - 1]
    grad_values = grad_ext[TAPS - 1:].astype(jnp.bfloat16)
    grad_tail = jnp.where(has_tail, grad_ext[:TAPS - 1], jnp.zeros_like(grad_ext[:TAPS - 1]))
    grad_w_out = jnp.dot(gated.T, grad_out, preferred_element_type=jnp.float32).astype(jnp.bfloat16)
    grad_w_val = jnp.dot(grad_values.T, normed, preferred_element_type=jnp.float32).astype(jnp.bfloat16)

    def add_block(total, index):
        start = (index * local_ch).astype(jnp.int32)
        grad_part = lax.dynamic_slice_in_dim(grad_values, start, local_ch, 1)
        weight_part = lax.dynamic_slice_in_dim(w_val, start, local_ch, 0)
        product = jnp.dot(grad_part, weight_part, preferred_element_type=jnp.float32)
        product = lax.optimization_barrier(product.astype(jnp.bfloat16)).astype(jnp.float32)
        return (total + product, None)
    grad_normed, _ = lax.scan(add_block, jnp.zeros((seq_len, D), jnp.float32), jnp.arange(N_TENSOR, dtype=jnp.int32))
    grad_gain = lax.optimization_barrier(jnp.sum(grad_normed * x_float * inv_rms, axis=0))
    scaled = gain * grad_normed
    grad_local = grad_out.astype(jnp.float32) + inv_rms * scaled - x_float * inv_rms ** 3 * lax.optimization_barrier(jnp.mean(scaled * x_float, axis=-1, keepdims=True))
    return (grad_local.astype(jnp.bfloat16), grad_w_val, grad_w_out, grad_filter, grad_tail, grad_gain)

def apply_section(section_args):
    return section_backward(*section_args)

def reference(x_in, grad_out, gain, w_val, w_out, filt, tail, micro_index):
    results = lax.map(apply_section, (x_in, grad_out, gain, w_val, w_out, filt, tail, micro_index))
    grad_local, grad_w_val, grad_w_out, grad_filter, grad_tail, grad_gain = results
    return (jnp.roll(grad_local, -1, axis=0), grad_w_val, grad_w_out, grad_filter, grad_tail, grad_gain)
```

```python
import functools

import jax
import jax.numpy as jnp
from jax import lax
from jax.experimental import pallas as pl
from jax.experimental.pallas import tpu as pltpu
from jax.sharding import PartitionSpec as P

TAPS = 3
EPSILON = 1e-06
MESH = pl.DeviceIdType.MESH
F32 = jnp.float32
BF16 = jnp.bfloat16


def dot_nt(left, right):
    return lax.dot_general(left, right, (((1,), (1,)), ((), ())), preferred_element_type=F32)


def dot_nn(left, right):
    return lax.dot_general(left, right, (((1,), (0,)), ((), ())), preferred_element_type=F32)


def kernel(
    n, sections, cuts, col_tile,
    x_ref, cot_ref, gain_ref, wv_hbm, wo_hbm, filt_ref, tail_ref, micro_ref,
    gin_out, gwv_out, gwo_out, gfilt_out, gtail_out, ggain_out,
    nrm, got, wv, wo, vals, gg, gat_t, gv, gv_t, gwo, gwv, part, sib, inc, outg, local, gparts, own,
    ag_send, ag_recv, own_sem, sib_send, sib_recv, line_send, line_recv,
    gain_send, gain_recv, load_sem, store_sem, shift_send, shift_recv,
):
    chips = n // 2
    rows = x_ref.shape[1]
    width = x_ref.shape[2]
    tokens = rows * n
    channels = wv.shape[0]
    wide = width // cuts
    me = lax.axis_index("tensor")
    sec = lax.axis_index("section")
    z = me // 2
    c = me % 2
    other = z * 2 + (1 - c)
    sec_prev = lax.rem(sec + sections - 1, sections)
    sec_next = lax.rem(sec + 1, sections)

    def rows_of(d):
        return pl.ds(pl.multiple_of(d * rows, rows), rows)

    load_cot = pltpu.make_async_copy(cot_ref.at[0], got.at[rows_of(me)], load_sem.at[0])
    load_wv = pltpu.make_async_copy(wv_hbm.at[0], wv, load_sem.at[1])
    load_wo = pltpu.make_async_copy(wo_hbm.at[0], wo, load_sem.at[2])
    load_cot.start()
    load_wo.start()
    load_wv.start()

    barrier = pltpu.get_barrier_semaphore()

    def greet(k, _):
        pl.semaphore_signal(
            barrier, inc=1, device_id={"tensor": lax.rem(me + k, n)}, device_id_type=MESH
        )
        return 0

    lax.fori_loop(1, n, greet, 0)
    pl.semaphore_signal(barrier, inc=1, device_id={"section": sec_prev}, device_id_type=MESH)
    pl.semaphore_signal(barrier, inc=1, device_id={"section": sec_next}, device_id_type=MESH)

    x_float = x_ref[0].astype(F32)
    inv_rms = lax.rsqrt(jnp.mean(x_float * x_float, axis=-1, keepdims=True) + EPSILON)
    nrm[rows_of(me), :] = (x_float * inv_rms * gain_ref[...]).astype(BF16)
    pl.semaphore_wait(barrier, n + 1)

    gathered = (got, nrm)

    def ag_copy(a, d, way, target):
        buf = gathered[a]
        return pltpu.make_async_remote_copy(
            src_ref=buf.at[rows_of(d)],
            dst_ref=buf.at[rows_of(d)],
            send_sem=ag_send.at[way, a, d],
            recv_sem=ag_recv.at[a, d],
            device_id={"tensor": target},
            device_id_type=MESH,
        )

    def ag_each(a, b, act):
        d = 2 * b + c

        @pl.when((b <= z) & (z < chips - 1))
        def _():
            act(ag_copy(a, d, 0, me + 2))

        @pl.when((b >= z) & (z > 0))
        def _():
            act(ag_copy(a, d, 1, me - 2))

        act(ag_copy(a, d, 2, other))

    def start(copy):
        copy.start()

    load_cot.wait()
    ag_each(0, z, start)
    ag_each(1, z, start)
    load_wo.wait()
    load_wv.wait()

    def project(b):
        d = 2 * b + (1 - c)
        pair = pl.ds(pl.multiple_of(b * 2 * rows, 2 * rows), 2 * rows)
        ag_copy(0, d, 2, other).wait_recv()
        gg[pair, :] = dot_nt(got[pair, :], wo[...])
        ag_copy(1, d, 2, other).wait_recv()
        vals[pair, :] = dot_nt(nrm[pair, :], wv[...]).astype(BF16).astype(F32)

    def project_at(s):
        @pl.when(z - s >= 0)
        def _():
            project(z - s)

        @pl.when(z + s < chips)
        def _():
            project(z + s)

    def ag_step(s, _):
        for a in range(2):

            @pl.when(z - s >= 0)
            def _():
                ag_copy(a, 2 * (z - s) + c, 0, me).wait_recv()
                ag_each(a, z - s, start)

            @pl.when(z + s < chips)
            def _():
                ag_copy(a, 2 * (z + s) + c, 1, me).wait_recv()
                ag_each(a, z + s, start)

            if a == 0:

                @pl.when(s == 1)
                def _():
                    project(z)

                @pl.when(s > 1)
                def _():
                    project_at(s - 1)

        return 0

    lax.fori_loop(1, chips, ag_step, 0)
    project_at(chips - 1)

    has_tail = (micro_ref[0] > 0).astype(F32)

    def strip(i, _):
        cs = pl.ds(pl.multiple_of(i * 128, 128), 128)
        v = vals[:, cs]
        f = [filt_ref[0, k : k + 1, cs] for k in range(TAPS)]
        lead = tail_ref[0, :, cs].astype(F32) * has_tail
        row = lax.broadcasted_iota(jnp.int32, (tokens, 128), 0)
        v1 = jnp.where(row == 0, lead[1:2], pltpu.roll(v, 1, 0))
        v2 = jnp.where(row == 0, lead[0:1], jnp.where(row == 1, lead[1:2], pltpu.roll(v, 2, 0)))
        conv = f[0] * v + f[1] * v1 + f[2] * v2
        sig = jax.nn.sigmoid(conv)
        gat_t[cs, :] = (conv * sig).T.astype(BF16)
        gc = gg[:, cs] * sig * (1.0 + conv * (1.0 - sig))
        gfilt_out[0, 0:1, cs] = jnp.sum(gc * v, axis=0, keepdims=True)
        gfilt_out[0, 1:2, cs] = jnp.sum(gc * v1, axis=0, keepdims=True)
        gfilt_out[0, 2:3, cs] = jnp.sum(gc * v2, axis=0, keepdims=True)
        gc1 = jnp.where(row == tokens - 1, 0.0, pltpu.roll(gc, tokens - 1, 0))
        gc2 = jnp.where(row >= tokens - 2, 0.0, pltpu.roll(gc, tokens - 2, 0))
        grad_values = f[0] * gc + f[1] * gc1 + f[2] * gc2
        gv[:, cs] = grad_values.astype(BF16)
        gv_t[cs, :] = grad_values.T.astype(BF16)
        gtail_out[0, 0:1, cs] = f[2] * gc[0:1] * has_tail
        gtail_out[0, 1:2, cs] = (f[1] * gc[0:1] + f[2] * gc[1:2]) * has_tail
        return 0

    lax.fori_loop(0, channels // 128, strip, 0)

    def sib_copy(q, b):
        return pltpu.make_async_remote_copy(
            src_ref=part.at[q, rows_of(2 * b + (1 - c))],
            dst_ref=sib.at[q, b],
            send_sem=sib_send.at[q, b],
            recv_sem=sib_recv.at[q, b],
            device_id={"tensor": other},
            device_id_type=MESH,
        )

    def line_copy(q, b, slot, target):
        return pltpu.make_async_remote_copy(
            src_ref=outg.at[q, b],
            dst_ref=inc.at[q, slot],
            send_sem=line_send.at[q, b],
            recv_sem=line_recv.at[q, slot],
            device_id={"tensor": target},
            device_id_type=MESH,
        )

    def share(q, _):
        cols = pl.ds(pl.multiple_of(q * wide, wide), wide)
        part[q] = dot_nn(gv[...], wv[:, cols]).astype(BF16)

        def send(b, _):
            sib_copy(q, b).start()
            return 0

        lax.fori_loop(0, chips, send, 0)
        return 0

    lax.fori_loop(0, cuts, share, 0)

    def chip_sum(q, b):
        sib_copy(q, b).wait_recv()
        return part[q, rows_of(2 * b + c), :].astype(F32) + sib[q, b].astype(F32)

    def rs_step(s):
        right = chips - 1 - s + z
        left = s - (chips - 1 - z)

        def piece(q, _):
            @pl.when((s >= z) & (right > z))
            def _():
                total = chip_sum(q, right)
                outg[q, right] = total.astype(BF16)

                @pl.when(z > 0)
                def _():
                    line_copy(q, right, right, me).wait_recv()
                    outg[q, right] = (total + inc[q, right].astype(F32)).astype(BF16)

                slot = jnp.where(right == z + 1, chips, right)
                line_copy(q, right, slot, me + 2).start()

            @pl.when((left >= 0) & (left < z))
            def _():
                total = chip_sum(q, left)
                outg[q, left] = total.astype(BF16)

                @pl.when(z < chips - 1)
                def _():
                    line_copy(q, left, left, me).wait_recv()
                    outg[q, left] = (total + inc[q, left].astype(F32)).astype(BF16)

                line_copy(q, left, left, me - 2).start()

            return 0

        lax.fori_loop(0, cuts, piece, 0)

    def gain_copy(k):
        return pltpu.make_async_remote_copy(
            src_ref=gparts.at[me],
            dst_ref=gparts.at[me],
            send_sem=gain_send.at[k],
            recv_sem=gain_recv.at[me],
            device_id={"tensor": lax.rem(me + k, n)},
            device_id_type=MESH,
        )

    def gain_arrival(k):
        d = lax.rem(me + k, n)
        return pltpu.make_async_remote_copy(
            src_ref=gparts.at[d],
            dst_ref=gparts.at[d],
            send_sem=gain_send.at[k],
            recv_sem=gain_recv.at[d],
            device_id={"tensor": d},
            device_id_type=MESH,
        )

    store_wo = pltpu.make_async_copy(gwo, gwo_out.at[0], store_sem.at[0])
    store_wv = pltpu.make_async_copy(gwv, gwv_out.at[0], store_sem.at[1])

    def weights_out():
        def tile(j, _):
            cols = pl.ds(pl.multiple_of(j * col_tile, col_tile), col_tile)
            gwo[:, cols] = dot_nn(gat_t[...], got[:, cols]).astype(BF16)
            return 0

        lax.fori_loop(0, width // col_tile, tile, 0)
        store_wo.start()

    def weights_val():
        def tile(j, _):
            cols = pl.ds(pl.multiple_of(j * col_tile, col_tile), col_tile)
            grad = dot_nn(gv_t[...], nrm[:, cols])
            gwv[:, cols] = grad.astype(BF16)
            own[:, cols] = (
                jnp.sum(grad * wv[:, cols].astype(F32), axis=0, keepdims=True) / gain_ref[:, cols]
            )
            return 0

        lax.fori_loop(0, width // col_tile, tile, 0)
        store_wv.start()
        gparts[me] = own[...]

        def send(k, _):
            gain_copy(k).start()
            return 0

        lax.fori_loop(1, n, send, 0)

    rs_step(0)
    weights_out()
    rs_step(1)
    weights_val()

    def rest(s, _):
        rs_step(s)
        return 0

    lax.fori_loop(2, chips - 1, rest, 0)

    def mine(q, dots):
        cols = pl.ds(pl.multiple_of(q * wide, wide), wide)
        local[:, cols] = chip_sum(q, z)

        @pl.when(z > 0)
        def _():
            line_copy(q, z, chips, me).wait_recv()
            local[:, cols] += inc[q, chips].astype(F32)

        @pl.when(z < chips - 1)
        def _():
            line_copy(q, z, z, me).wait_recv()
            local[:, cols] += inc[q, z].astype(F32)

        scaled = local[:, cols] * gain_ref[:, cols]
        local[:, cols] = scaled
        return dots + jnp.sum(scaled * x_ref[0, :, cols].astype(F32), axis=-1, keepdims=True)

    dots = lax.fori_loop(0, cuts, mine, jnp.zeros((rows, 1), F32))
    factor = inv_rms**3 * (dots / width)
    outgoing = nrm.at[rows_of(me)]

    def ag_drain(b, _):
        for a in range(2):
            ag_each(a, b, lambda copy: copy.wait_send())
        return 0

    lax.fori_loop(0, chips, ag_drain, 0)
    outgoing[...] = (
        cot_ref[0].astype(F32) + inv_rms * local[...] - x_ref[0].astype(F32) * factor
    ).astype(BF16)
    shift = pltpu.make_async_remote_copy(
        src_ref=outgoing,
        dst_ref=gin_out.at[0],
        send_sem=shift_send,
        recv_sem=shift_recv,
        device_id={"section": sec_prev},
        device_id_type=MESH,
    )
    shift.start()

    def gain_wait(k, _):
        gain_arrival(k).wait_recv()
        gain_copy(k).wait_send()
        return 0

    lax.fori_loop(1, n, gain_wait, 0)
    ggain_out[...] = jnp.sum(gparts[...], axis=0)

    def rs_drain(i, _):
        q, b = i // chips, i % chips
        sib_copy(q, b).wait_send()

        @pl.when(b != z)
        def _():
            line_copy(q, b, b, me).wait_send()

        return 0

    lax.fori_loop(0, cuts * chips, rs_drain, 0)
    store_wo.wait()
    store_wv.wait()
    shift.wait()


def on_device(n, sections, x_in, grad_out, gain, w_val, w_out, filt, tail, micro_index):
    _, rows, width = x_in.shape
    channels = w_val.shape[1]
    chips = n // 2
    tokens = rows * n
    cuts = 4
    wide = width // cuts
    vmem = pl.BlockSpec(memory_space=pltpu.VMEM)
    hbm = pl.BlockSpec(memory_space=pl.ANY)
    dma = pltpu.SemaphoreType.DMA
    return pl.pallas_call(
        functools.partial(kernel, n, sections, cuts, 512),
        out_shape=(
            jax.ShapeDtypeStruct(x_in.shape, BF16),
            jax.ShapeDtypeStruct(w_val.shape, BF16),
            jax.ShapeDtypeStruct(w_out.shape, BF16),
            jax.ShapeDtypeStruct(filt.shape, F32),
            jax.ShapeDtypeStruct(tail.shape, F32),
            jax.ShapeDtypeStruct(gain.shape, F32),
        ),
        in_specs=[vmem, vmem, vmem, hbm, hbm, vmem, vmem, pl.BlockSpec(memory_space=pltpu.SMEM)],
        out_specs=(hbm, hbm, hbm, vmem, vmem, vmem),
        scratch_shapes=[
            pltpu.VMEM((tokens, width), BF16),
            pltpu.VMEM((tokens, width), BF16),
            pltpu.VMEM((channels, width), BF16),
            pltpu.VMEM((channels, width), BF16),
            pltpu.VMEM((tokens, channels), F32),
            pltpu.VMEM((tokens, channels), F32),
            pltpu.VMEM((channels, tokens), BF16),
            pltpu.VMEM((tokens, channels), BF16),
            pltpu.VMEM((channels, tokens), BF16),
            pltpu.VMEM((channels, width), BF16),
            pltpu.VMEM((channels, width), BF16),
            pltpu.VMEM((cuts, tokens, wide), BF16),
            pltpu.VMEM((cuts, chips, rows, wide), BF16),
            pltpu.VMEM((cuts, chips + 1, rows, wide), BF16),
            pltpu.VMEM((cuts, chips, rows, wide), BF16),
            pltpu.VMEM((rows, width), F32),
            pltpu.VMEM((n, 1, width), F32),
            pltpu.VMEM((1, width), F32),
            dma((3, 2, n)),
            dma((2, n)),
            dma,
            dma((cuts, chips)),
            dma((cuts, chips)),
            dma((cuts, chips)),
            dma((cuts, chips + 1)),
            dma((n,)),
            dma((n,)),
            dma((3,)),
            dma((2,)),
            dma,
            dma,
        ],
        compiler_params=pltpu.CompilerParams(
            collective_id=0, has_side_effects=True, vmem_limit_bytes=60 * 2**20
        ),
    )(x_in, grad_out, gain, w_val, w_out, filt, tail, micro_index)


def solution(mesh):
    placed = (
        P("section", "tensor", None),
        P("section", "tensor", None),
        P("section", None),
        P("section", "tensor", None),
        P("section", "tensor", None),
        P("section", None, "tensor"),
        P("section", None, "tensor"),
        P("section"),
    )
    return jax.shard_map(
        functools.partial(on_device, mesh.shape["tensor"], mesh.shape["section"]),
        mesh=mesh,
        in_specs=placed,
        out_specs=(
            P("section", "tensor", None),
            P("section", "tensor", None),
            P("section", "tensor", None),
            P("section", None, "tensor"),
            P("section", None, "tensor"),
            P("section", None),
        ),
        check_vma=False,
    )
```

```python
import functools

import jax
import jax.numpy as jnp
from jax import lax
from jax.experimental import pallas as pl
from jax.experimental.pallas import tpu as pltpu
from jax.sharding import PartitionSpec as P

TAPS = 3
EPSILON = 1e-06
MESH = pl.DeviceIdType.MESH
F32 = jnp.float32
BF16 = jnp.bfloat16


def dot_nt(left, right):
    return lax.dot_general(left, right, (((1,), (1,)), ((), ())), preferred_element_type=F32)


def dot_nn(left, right):
    return lax.dot_general(left, right, (((1,), (0,)), ((), ())), preferred_element_type=F32)


def kernel(
    n, col_tile,
    x_ref, cot_ref, gain_ref, wv_hbm, wo_hbm, filt_ref, tail_ref, micro_ref,
    gloc_out, nrm_out, got_out, gat_t, gv_t, gfilt_out, gtail_out, ggain_out,
    nrm, got, wv, wo, vals, gg, gat, gv, part, sib, inc, outg, gparts, own,
    ag_send, ag_recv, sib_send, sib_recv, line_send, line_recv,
    gain_send, gain_recv, load_sem, store_sem,
):
    chips = n // 2
    rows = x_ref.shape[1]
    width = x_ref.shape[2]
    tokens = rows * n
    channels = wv.shape[0]
    height = 16
    cuts = rows // height
    hop = 2
    last = chips - 1
    me = lax.axis_index("tensor")
    z = me // 2
    c = me % 2
    other = z * 2 + (1 - c)

    def rows_of(d):
        return pl.ds(pl.multiple_of(d * rows, rows), rows)

    def piece_of(q):
        return pl.ds(pl.multiple_of(q * height, height), height)

    load_cot = pltpu.make_async_copy(cot_ref.at[0], got.at[rows_of(me)], load_sem.at[0])
    load_wv = pltpu.make_async_copy(wv_hbm.at[0], wv, load_sem.at[1])
    load_wo = pltpu.make_async_copy(wo_hbm.at[0], wo, load_sem.at[2])
    load_cot.start()
    load_wo.start()
    load_wv.start()

    barrier = pltpu.get_barrier_semaphore()

    def greet(k, _):
        pl.semaphore_signal(
            barrier, inc=1, device_id={"tensor": lax.rem(me + k, n)}, device_id_type=MESH
        )
        return 0

    lax.fori_loop(1, n, greet, 0)

    x_float = x_ref[0].astype(F32)
    inv_rms = lax.rsqrt(jnp.mean(x_float * x_float, axis=-1, keepdims=True) + EPSILON)
    nrm[rows_of(me), :] = (x_float * inv_rms * gain_ref[...]).astype(BF16)

    has_tail = (micro_ref[0] > 0).astype(F32)
    vals[0:8, :] = jnp.zeros((8, channels), F32)
    vals[6:8, :] = tail_ref[0].astype(F32) * has_tail
    vals[tokens + 8 : tokens + 16, :] = jnp.zeros((8, channels), F32)
    gg[tokens : tokens + 8, :] = jnp.zeros((8, channels), F32)
    gfilt_out[...] = jnp.zeros_like(gfilt_out)
    pl.semaphore_wait(barrier, n - 1)

    gathered = (got, nrm)

    def ag_copy(a, d, way, target):
        buf = gathered[a]
        return pltpu.make_async_remote_copy(
            src_ref=buf.at[rows_of(d)],
            dst_ref=buf.at[rows_of(d)],
            send_sem=ag_send.at[way, a, d],
            recv_sem=ag_recv.at[a, d],
            device_id={"tensor": target},
            device_id_type=MESH,
        )

    def ag_each(a, b, act):
        d = 2 * b + c

        @pl.when((b <= z) & (z < last))
        def _():
            act(ag_copy(a, d, 0, me + 2))

        @pl.when((b >= z) & (z > 0))
        def _():
            act(ag_copy(a, d, 1, me - 2))

        act(ag_copy(a, d, 2, other))

    def start(copy):
        copy.start()

    load_cot.wait()
    ag_each(0, z, start)
    ag_each(1, z, start)
    load_wo.wait()
    load_wv.wait()

    def project(a, b):
        ag_copy(a, 2 * b + (1 - c), 2, other).wait_recv()
        first = pl.multiple_of(b * 2 * rows, 2 * rows)
        pair = pl.ds(first, 2 * rows)
        if a == 0:
            gg[pair, :] = dot_nt(got[pair, :], wo[...])
        else:
            vals[pl.ds(pl.multiple_of(first + 8, 8), 2 * rows), :] = (
                dot_nt(nrm[pair, :], wv[...]).astype(BF16).astype(F32)
            )

    def project_at(a, s):
        @pl.when(z - s >= 0)
        def _():
            project(a, z - s)

        @pl.when((z + s < chips) & (s > 0))
        def _():
            project(a, z + s)

    def sib_copy(b):
        return pltpu.make_async_remote_copy(
            src_ref=part.at[rows_of(2 * b + (1 - c))],
            dst_ref=sib.at[b],
            send_sem=sib_send.at[b],
            recv_sem=sib_recv.at[b],
            device_id={"tensor": other},
            device_id_type=MESH,
        )

    def share(d, _):
        first = pl.multiple_of(d * rows, rows)

        def strip(i, _):
            cs = pl.ds(pl.multiple_of(i * 128, 128), 128)
            window = vals[pl.ds(first, rows + 16), cs]
            f = [filt_ref[0, k : k + 1, cs] for k in range(TAPS)]
            v = window[8:]
            v1 = pltpu.roll(window, 1, 0)[8:]
            v2 = pltpu.roll(window, 2, 0)[8:]
            conv = f[0] * v + f[1] * v1 + f[2] * v2
            sig = jax.nn.sigmoid(conv)
            gat[rows_of(d), cs] = (conv * sig)[:rows].astype(BF16)
            gc = gg[pl.ds(first, rows + 8), cs] * sig * (1.0 + conv * (1.0 - sig))
            gc1 = pltpu.roll(gc, rows + 7, 0)[:rows]
            gc2 = pltpu.roll(gc, rows + 6, 0)[:rows]
            here = gc[:rows]
            for k, shifted in enumerate((v, v1, v2)):
                gfilt_out[0, k : k + 1, cs] += jnp.sum(here * shifted[:rows], axis=0, keepdims=True)
            gv[rows_of(d), cs] = (f[0] * here + f[1] * gc1 + f[2] * gc2).astype(BF16)

            @pl.when(d == 0)
            def _():
                gtail_out[0, 0:1, cs] = f[2] * gc[0:1] * has_tail
                gtail_out[0, 1:2, cs] = (f[1] * gc[0:1] + f[2] * gc[1:2]) * has_tail

            return 0

        lax.fori_loop(0, channels // 128, strip, 0)

        def tile(j, _):
            cols = pl.ds(pl.multiple_of(j * col_tile, col_tile), col_tile)
            part[rows_of(d), cols] = dot_nn(gv[rows_of(d), :], wv[:, cols]).astype(BF16)
            return 0

        lax.fori_loop(0, width // col_tile, tile, 0)

        @pl.when(d % 2 != c)
        def _():
            sib_copy(d // 2).start()

        return 0

    def low_end(s):
        lo = z - s
        return jnp.where(lo > 0, 2 * lo + 1, 0)

    def high_end(s):
        hi = z + s
        return jnp.where(hi < last, 2 * hi + 1, n)

    def line_copy(q, b, slot, target):
        return pltpu.make_async_remote_copy(
            src_ref=outg.at[b, piece_of(q)],
            dst_ref=inc.at[slot, piece_of(q)],
            send_sem=line_send.at[q, b],
            recv_sem=line_recv.at[q, slot],
            device_id={"tensor": target},
            device_id_type=MESH,
        )

    def chip_sum(q, b):
        mine = pl.ds(pl.multiple_of((2 * b + c) * rows + q * height, height), height)
        return part[mine, :].astype(F32) + sib[b, piece_of(q), :].astype(F32)

    def forward(q, b, slot, target, upstream):
        @pl.when(q == 0)
        def _():
            sib_copy(b).wait_recv()

        @pl.when(upstream)
        def _():
            line_copy(q, b, b, me).wait_recv()
            outg[b, piece_of(q), :] = (
                chip_sum(q, b) + inc[b, piece_of(q), :].astype(F32)
            ).astype(BF16)

        @pl.when(jnp.logical_not(upstream))
        def _():
            outg[b, piece_of(q), :] = chip_sum(q, b).astype(BF16)

        line_copy(q, b, slot, target).start()

    def order(i, late):
        return jnp.where((late == 1) & (i >= last - 1), 2 * last - 1 - i, i)

    def right_at(t):
        u = t - hop * z
        b = order(u // cuts, c)

        @pl.when((u >= cuts) & (u < cuts * chips) & (b > z))
        def _():
            forward(u % cuts, b, jnp.where(b == z + 1, chips, b), me + 2, z > 0)

    def left_at(t):
        u = t - hop * (last - z)
        b = last - order(u // cuts, 1 - c)

        @pl.when((u >= cuts) & (u < cuts * chips) & (b < z))
        def _():
            forward(u % cuts, b, b, me - 2, z < last)

    def windows(s):
        def turn(q, _):
            right_at((s - c) * cuts + q)
            left_at((s - (1 - c)) * cuts + q)
            return 0

        lax.fori_loop(0, cuts, turn, 0)

    def shares(s, low, high):
        lax.fori_loop(low_end(s), low, share, 0)
        lax.fori_loop(high, high_end(s), share, 0)

    def gain_copy(k, d):
        return pltpu.make_async_remote_copy(
            src_ref=gparts.at[d],
            dst_ref=gparts.at[d],
            send_sem=gain_send.at[k],
            recv_sem=gain_recv.at[d],
            device_id={"tensor": lax.rem(me + k, n)},
            device_id_type=MESH,
        )

    store_nrm = pltpu.make_async_copy(nrm, nrm_out, store_sem.at[0])
    store_got = pltpu.make_async_copy(got, got_out, store_sem.at[1])

    def gain_part():
        store_nrm.start()
        store_got.start()

        def turned(i, _):
            cs = pl.ds(pl.multiple_of(i * 128, 128), 128)
            gat_t[cs, :] = gat[:, cs].astype(F32).T.astype(BF16)
            gv_t[cs, :] = gv[:, cs].astype(F32).T.astype(BF16)
            return 0

        lax.fori_loop(0, channels // 128, turned, 0)

        def tile(j, _):
            cols = pl.ds(pl.multiple_of(j * col_tile, col_tile), col_tile)
            grad = dot_nn(gv_t[...], nrm[:, cols])
            own[:, cols] = (
                jnp.sum(grad * wv[:, cols].astype(F32), axis=0, keepdims=True) / gain_ref[:, cols]
            )
            return 0

        lax.fori_loop(0, width // col_tile, tile, 0)
        gparts[me] = own[...]

        def send(k, _):
            gain_copy(k, me).start()
            return 0

        lax.fori_loop(1, n, send, 0)

    def process(s, low, high):
        project_at(1, s)
        shares(s, low, high)
        windows(s)

    inner = (z > 0) & (z < last)
    project_at(0, 0)
    process(0, 2 * z + 1, 2 * z + 1)

    def ag_step(s, _):
        for a in range(2):

            @pl.when(z - s >= 0)
            def _():
                ag_copy(a, 2 * (z - s) + c, 0, me).wait_recv()
                ag_each(a, z - s, start)

            @pl.when(z + s < chips)
            def _():
                ag_copy(a, 2 * (z + s) + c, 1, me).wait_recv()
                ag_each(a, z + s, start)

            if a == 0:
                project_at(0, s)

        process(s, low_end(s - 1), high_end(s - 1))

        @pl.when((s == last - 1) & inner)
        def _():
            gain_part()

        return 0

    lax.fori_loop(1, chips, ag_step, 0)

    def rest(t, _):
        right_at(t + (1 - c) * cuts)
        left_at(t + c * cuts)
        return 0

    lax.fori_loop(cuts * last, cuts * chips + hop * chips, rest, 0)

    @pl.when(jnp.logical_not(inner))
    def _():
        gain_part()

    sib_copy(z).wait_recv()

    def finish(q, _):
        @pl.when(z > 0)
        def _():
            line_copy(q, z, chips, me).wait_recv()

        @pl.when(z < last)
        def _():
            line_copy(q, z, z, me).wait_recv()

        from_left = jnp.where(z > 0, inc[chips, piece_of(q), :].astype(F32), 0.0)
        from_right = jnp.where(z < last, inc[z, piece_of(q), :].astype(F32), 0.0)
        scaled = (chip_sum(q, z) + from_left + from_right) * gain_ref[...]
        x_now = x_ref[0, piece_of(q), :].astype(F32)
        inv = lax.rsqrt(jnp.mean(x_now * x_now, axis=-1, keepdims=True) + EPSILON)
        dots = jnp.mean(scaled * x_now, axis=-1, keepdims=True)
        gloc_out[piece_of(q), :] = (
            cot_ref[0, piece_of(q), :].astype(F32) + inv * scaled - x_now * (inv**3 * dots)
        ).astype(BF16)
        return 0

    lax.fori_loop(0, cuts, finish, 0)

    def gain_wait(k, _):
        gain_copy(k, lax.rem(me + k, n)).wait_recv()
        gain_copy(k, me).wait_send()
        return 0

    lax.fori_loop(1, n, gain_wait, 0)
    ggain_out[...] = jnp.sum(gparts[...], axis=0)

    def ag_drain(b, _):
        for a in range(2):
            ag_each(a, b, lambda copy: copy.wait_send())
        sib_copy(b).wait_send()
        return 0

    lax.fori_loop(0, chips, ag_drain, 0)

    def line_drain(i, _):
        q, b = i // chips, i % chips

        @pl.when(b != z)
        def _():
            line_copy(q, b, b, me).wait_send()

        return 0

    lax.fori_loop(0, cuts * chips, line_drain, 0)
    store_nrm.wait()
    store_got.wait()


def on_device(n, sections, x_in, grad_out, gain, w_val, w_out, filt, tail, micro_index):
    _, rows, width = x_in.shape
    channels = w_val.shape[1]
    chips = n // 2
    tokens = rows * n
    cuts = rows // 16
    vmem = pl.BlockSpec(memory_space=pltpu.VMEM)
    hbm = pl.BlockSpec(memory_space=pl.ANY)
    dma = pltpu.SemaphoreType.DMA
    grad_local, normed, cot, gat_t, gv_t, grad_filter, grad_tail, grad_gain = pl.pallas_call(
        functools.partial(kernel, n, 512),
        out_shape=(
            jax.ShapeDtypeStruct((rows, width), BF16),
            jax.ShapeDtypeStruct((tokens, width), BF16),
            jax.ShapeDtypeStruct((tokens, width), BF16),
            jax.ShapeDtypeStruct((channels, tokens), BF16),
            jax.ShapeDtypeStruct((channels, tokens), BF16),
            jax.ShapeDtypeStruct(filt.shape, F32),
            jax.ShapeDtypeStruct(tail.shape, F32),
            jax.ShapeDtypeStruct(gain.shape, F32),
        ),
        in_specs=[vmem, vmem, vmem, hbm, hbm, vmem, vmem, pl.BlockSpec(memory_space=pltpu.SMEM)],
        out_specs=(vmem, hbm, hbm, vmem, vmem, vmem, vmem, vmem),
        scratch_shapes=[
            pltpu.VMEM((tokens, width), BF16),
            pltpu.VMEM((tokens, width), BF16),
            pltpu.VMEM((channels, width), BF16),
            pltpu.VMEM((channels, width), BF16),
            pltpu.VMEM((tokens + 16, channels), F32),
            pltpu.VMEM((tokens + 8, channels), F32),
            pltpu.VMEM((tokens, channels), BF16),
            pltpu.VMEM((tokens, channels), BF16),
            pltpu.VMEM((tokens, width), BF16),
            pltpu.VMEM((chips, rows, width), BF16),
            pltpu.VMEM((chips + 1, rows, width), BF16),
            pltpu.VMEM((chips, rows, width), BF16),
            pltpu.VMEM((n, 1, width), F32),
            pltpu.VMEM((1, width), F32),
            dma((3, 2, n)),
            dma((2, n)),
            dma((chips,)),
            dma((chips,)),
            dma((cuts, chips)),
            dma((cuts, chips + 1)),
            dma((n,)),
            dma((n,)),
            dma((3,)),
            dma((2,)),
        ],
        compiler_params=pltpu.CompilerParams(
            collective_id=0, has_side_effects=True, vmem_limit_bytes=60 * 2**20
        ),
    )(x_in, grad_out, gain, w_val, w_out, filt, tail, micro_index)
    route = [(i, (i - 1) % sections) for i in range(sections)]
    received = lax.ppermute(grad_local, "section", route)
    return (
        received[None],
        dot_nn(gv_t, normed).astype(BF16)[None],
        dot_nn(gat_t, cot).astype(BF16)[None],
        grad_filter,
        grad_tail,
        grad_gain,
    )


def solution(mesh):
    placed = (
        P("section", "tensor", None),
        P("section", "tensor", None),
        P("section", None),
        P("section", "tensor", None),
        P("section", "tensor", None),
        P("section", None, "tensor"),
        P("section", None, "tensor"),
        P("section"),
    )
    return jax.shard_map(
        functools.partial(on_device, mesh.shape["tensor"], mesh.shape["section"]),
        mesh=mesh,
        in_specs=placed,
        out_specs=(
            P("section", "tensor", None),
            P("section", "tensor", None),
            P("section", "tensor", None),
            P("section", None, "tensor"),
            P("section", None, "tensor"),
            P("section", None),
        ),
        check_vma=False,
    )
```

```python
import functools

import jax
import jax.numpy as jnp
from jax import lax
from jax.experimental import pallas as pl
from jax.experimental.pallas import tpu as pltpu
from jax.sharding import PartitionSpec as P

TAPS = 3
EPSILON = 1e-06
MESH = pl.DeviceIdType.MESH
F32 = jnp.float32
BF16 = jnp.bfloat16


def dot_nt(left, right):
    return lax.dot_general(left, right, (((1,), (1,)), ((), ())), preferred_element_type=F32)


def dot_nn(left, right):
    return lax.dot_general(left, right, (((1,), (0,)), ((), ())), preferred_element_type=F32)


def kernel(
    n, sections, col_tile,
    x_ref, cot_ref, gain_ref, wv_hbm, wo_hbm, filt_ref, tail_ref, micro_ref,
    gin_out, gwv_out, gwo_out, gfilt_out, gtail_out, ggain_out,
    nrm, got, wv, wo, vals, gg, gat, gv, gat_t, gv_t, gwo, gwv, gloc, part, sib, inc, outg, gparts, own,
    ag_send, ag_recv, sib_send, sib_recv, line_send, line_recv,
    gain_send, gain_recv, load_sem, store_sem, shift_send, shift_recv,
):
    chips = n // 2
    rows = x_ref.shape[1]
    width = x_ref.shape[2]
    tokens = rows * n
    channels = wv.shape[0]
    height = 16
    cuts = rows // height
    hop = 2
    last = chips - 1
    me = lax.axis_index("tensor")
    z = me // 2
    c = me % 2
    other = z * 2 + (1 - c)
    sec = lax.axis_index("section")
    sec_prev = lax.rem(sec + sections - 1, sections)
    sec_next = lax.rem(sec + 1, sections)

    def rows_of(d):
        return pl.ds(pl.multiple_of(d * rows, rows), rows)

    def piece_of(q):
        return pl.ds(pl.multiple_of(q * height, height), height)

    load_cot = pltpu.make_async_copy(cot_ref.at[0], got.at[rows_of(me)], load_sem.at[0])
    load_wv = pltpu.make_async_copy(wv_hbm.at[0], wv, load_sem.at[1])
    load_wo = pltpu.make_async_copy(wo_hbm.at[0], wo, load_sem.at[2])
    load_cot.start()
    load_wo.start()
    load_wv.start()

    barrier = pltpu.get_barrier_semaphore()

    def greet(k, _):
        pl.semaphore_signal(
            barrier, inc=1, device_id={"tensor": lax.rem(me + k, n)}, device_id_type=MESH
        )
        return 0

    lax.fori_loop(1, n, greet, 0)
    pl.semaphore_signal(barrier, inc=1, device_id={"section": sec_prev}, device_id_type=MESH)
    pl.semaphore_signal(barrier, inc=1, device_id={"section": sec_next}, device_id_type=MESH)

    x_float = x_ref[0].astype(F32)
    inv_rms = lax.rsqrt(jnp.mean(x_float * x_float, axis=-1, keepdims=True) + EPSILON)
    nrm[rows_of(me), :] = (x_float * inv_rms * gain_ref[...]).astype(BF16)

    has_tail = (micro_ref[0] > 0).astype(F32)
    vals[0:8, :] = jnp.zeros((8, channels), F32)
    vals[6:8, :] = tail_ref[0].astype(F32) * has_tail
    vals[tokens + 8 : tokens + 16, :] = jnp.zeros((8, channels), F32)
    gg[tokens : tokens + 8, :] = jnp.zeros((8, channels), F32)
    gfilt_out[...] = jnp.zeros_like(gfilt_out)
    pl.semaphore_wait(barrier, n + 1)

    gathered = (got, nrm)

    def ag_copy(a, d, way, target):
        buf = gathered[a]
        return pltpu.make_async_remote_copy(
            src_ref=buf.at[rows_of(d)],
            dst_ref=buf.at[rows_of(d)],
            send_sem=ag_send.at[way, a, d],
            recv_sem=ag_recv.at[a, d],
            device_id={"tensor": target},
            device_id_type=MESH,
        )

    def ag_each(a, b, act):
        d = 2 * b + c

        @pl.when((b <= z) & (z < last))
        def _():
            act(ag_copy(a, d, 0, me + 2))

        @pl.when((b >= z) & (z > 0))
        def _():
            act(ag_copy(a, d, 1, me - 2))

        act(ag_copy(a, d, 2, other))

    def start(copy):
        copy.start()

    load_cot.wait()
    ag_each(0, z, start)
    ag_each(1, z, start)
    load_wo.wait()
    load_wv.wait()

    def project(a, b):
        ag_copy(a, 2 * b + (1 - c), 2, other).wait_recv()
        first = pl.multiple_of(b * 2 * rows, 2 * rows)
        pair = pl.ds(first, 2 * rows)
        if a == 0:
            gg[pair, :] = dot_nt(got[pair, :], wo[...])
        else:
            vals[pl.ds(pl.multiple_of(first + 8, 8), 2 * rows), :] = (
                dot_nt(nrm[pair, :], wv[...]).astype(BF16).astype(F32)
            )

    def project_at(a, s):
        @pl.when(z - s >= 0)
        def _():
            project(a, z - s)

        @pl.when((z + s < chips) & (s > 0))
        def _():
            project(a, z + s)

    def sib_copy(b):
        return pltpu.make_async_remote_copy(
            src_ref=part.at[rows_of(2 * b + (1 - c))],
            dst_ref=sib.at[b],
            send_sem=sib_send.at[b],
            recv_sem=sib_recv.at[b],
            device_id={"tensor": other},
            device_id_type=MESH,
        )

    def share(d, _):
        first = pl.multiple_of(d * rows, rows)

        def strip(i, _):
            cs = pl.ds(pl.multiple_of(i * 128, 128), 128)
            window = vals[pl.ds(first, rows + 16), cs]
            f = [filt_ref[k, :, cs] for k in range(TAPS)]
            v = window[8:]
            v1 = pltpu.roll(window, 1, 0)[8:]
            v2 = pltpu.roll(window, 2, 0)[8:]
            conv = f[0] * v + f[1] * v1 + f[2] * v2
            sig = jax.nn.sigmoid(conv)
            gat[rows_of(d), cs] = (conv * sig)[:rows].astype(BF16)
            gc = gg[pl.ds(first, rows + 8), cs] * sig * (1.0 + conv * (1.0 - sig))
            gc1 = pltpu.roll(gc, rows + 7, 0)[:rows]
            gc2 = pltpu.roll(gc, rows + 6, 0)[:rows]
            here = gc[:rows]
            for k, shifted in enumerate((v, v1, v2)):
                gfilt_out[k, :, cs] += jnp.sum(here * shifted[:rows], axis=0, keepdims=True)
            gv[rows_of(d), cs] = (f[0] * here + f[1] * gc1 + f[2] * gc2).astype(BF16)

            @pl.when(d == 0)
            def _():
                gtail_out[0, 0:1, cs] = f[2] * gc[0:1] * has_tail
                gtail_out[0, 1:2, cs] = (f[1] * gc[0:1] + f[2] * gc[1:2]) * has_tail

            return 0

        lax.fori_loop(0, channels // 128, strip, 0)

        def tile(j, _):
            cols = pl.ds(pl.multiple_of(j * col_tile, col_tile), col_tile)
            part[rows_of(d), cols] = dot_nn(gv[rows_of(d), :], wv[:, cols]).astype(BF16)
            return 0

        lax.fori_loop(0, width // col_tile, tile, 0)

        @pl.when(d % 2 != c)
        def _():
            sib_copy(d // 2).start()

        return 0

    def low_end(s):
        lo = z - s
        return jnp.where(lo > 0, 2 * lo + 1, 0)

    def high_end(s):
        hi = z + s
        return jnp.where(hi < last, 2 * hi + 1, n)

    def line_copy(q, b, slot, target):
        return pltpu.make_async_remote_copy(
            src_ref=outg.at[b, piece_of(q)],
            dst_ref=inc.at[slot, piece_of(q)],
            send_sem=line_send.at[q, b],
            recv_sem=line_recv.at[q, slot],
            device_id={"tensor": target},
            device_id_type=MESH,
        )

    def chip_sum(q, b):
        mine = pl.ds(pl.multiple_of((2 * b + c) * rows + q * height, height), height)
        return part[mine, :].astype(F32) + sib[b, piece_of(q), :].astype(F32)

    def forward(q, b, slot, target, upstream):
        @pl.when(q == 0)
        def _():
            sib_copy(b).wait_recv()

        @pl.when(upstream)
        def _():
            line_copy(q, b, b, me).wait_recv()
            outg[b, piece_of(q), :] = (
                chip_sum(q, b) + inc[b, piece_of(q), :].astype(F32)
            ).astype(BF16)

        @pl.when(jnp.logical_not(upstream))
        def _():
            outg[b, piece_of(q), :] = chip_sum(q, b).astype(BF16)

        line_copy(q, b, slot, target).start()

    def order(i, late):
        return jnp.where((late == 1) & (i >= last - 1), 2 * last - 1 - i, i)

    def right_at(t):
        u = t - hop * z
        b = order(u // cuts, c)

        @pl.when((u >= cuts) & (u < cuts * chips) & (b > z))
        def _():
            forward(u % cuts, b, jnp.where(b == z + 1, chips, b), me + 2, z > 0)

    def left_at(t):
        u = t - hop * (last - z)
        b = last - order(u // cuts, 1 - c)

        @pl.when((u >= cuts) & (u < cuts * chips) & (b < z))
        def _():
            forward(u % cuts, b, b, me - 2, z < last)

    def windows(s):
        def turn(q, _):
            right_at((s - c) * cuts + q)
            left_at((s - (1 - c)) * cuts + q)
            return 0

        lax.fori_loop(0, cuts, turn, 0)

    def shares(s, low, high):
        lax.fori_loop(low_end(s), low, share, 0)
        lax.fori_loop(high, high_end(s), share, 0)

    def gain_copy(k, d):
        return pltpu.make_async_remote_copy(
            src_ref=gparts.at[d],
            dst_ref=gparts.at[d],
            send_sem=gain_send.at[k],
            recv_sem=gain_recv.at[d],
            device_id={"tensor": lax.rem(me + k, n)},
            device_id_type=MESH,
        )

    store_wo = pltpu.make_async_copy(gwo, gwo_out, store_sem.at[0])
    store_wv = pltpu.make_async_copy(gwv, gwv_out, store_sem.at[1])

    def gain_part():
        def turned(i, _):
            cs = pl.ds(pl.multiple_of(i * 128, 128), 128)
            gat_t[cs, :] = gat[:, cs].astype(F32).T.astype(BF16)
            gv_t[cs, :] = gv[:, cs].astype(F32).T.astype(BF16)
            return 0

        lax.fori_loop(0, channels // 128, turned, 0)

        def tile(j, _):
            cols = pl.ds(pl.multiple_of(j * col_tile, col_tile), col_tile)
            grad = dot_nn(gv_t[...], nrm[:, cols])
            gwv[:, cols] = grad.astype(BF16)
            own[:, cols] = (
                jnp.sum(grad * wv[:, cols].astype(F32), axis=0, keepdims=True) / gain_ref[:, cols]
            )
            return 0

        lax.fori_loop(0, width // col_tile, tile, 0)
        store_wv.start()
        gparts[me] = own[...]

        def send(k, _):
            gain_copy(k, me).start()
            return 0

        lax.fori_loop(1, n, send, 0)

        def out_tile(j, _):
            cols = pl.ds(pl.multiple_of(j * col_tile, col_tile), col_tile)
            gwo[:, cols] = dot_nn(gat_t[...], got[:, cols]).astype(BF16)
            return 0

        lax.fori_loop(0, width // col_tile, out_tile, 0)
        store_wo.start()

    def process(s, low, high):
        project_at(1, s)
        shares(s, low, high)
        windows(s)

    inner = (z > 0) & (z < last)
    project_at(0, 0)
    process(0, 2 * z + 1, 2 * z + 1)

    def ag_step(s, _):
        for a in range(2):

            @pl.when(z - s >= 0)
            def _():
                ag_copy(a, 2 * (z - s) + c, 0, me).wait_recv()
                ag_each(a, z - s, start)

            @pl.when(z + s < chips)
            def _():
                ag_copy(a, 2 * (z + s) + c, 1, me).wait_recv()
                ag_each(a, z + s, start)

            if a == 0:
                project_at(0, s)

        process(s, low_end(s - 1), high_end(s - 1))

        @pl.when((s == last - 1) & inner)
        def _():
            gain_part()

        return 0

    lax.fori_loop(1, chips, ag_step, 0)

    def rest(t, _):
        right_at(t + (1 - c) * cuts)
        left_at(t + c * cuts)
        return 0

    lax.fori_loop(cuts * last, cuts * chips + hop * chips, rest, 0)

    @pl.when(jnp.logical_not(inner))
    def _():
        gain_part()

    def shift_copy(q):
        return pltpu.make_async_remote_copy(
            src_ref=gloc.at[piece_of(q)],
            dst_ref=gin_out.at[piece_of(q)],
            send_sem=shift_send.at[q],
            recv_sem=shift_recv.at[q],
            device_id={"section": sec_prev},
            device_id_type=MESH,
        )

    sib_copy(z).wait_recv()

    def finish(q, _):
        @pl.when(z > 0)
        def _():
            line_copy(q, z, chips, me).wait_recv()

        @pl.when(z < last)
        def _():
            line_copy(q, z, z, me).wait_recv()

        from_left = jnp.where(z > 0, inc[chips, piece_of(q), :].astype(F32), 0.0)
        from_right = jnp.where(z < last, inc[z, piece_of(q), :].astype(F32), 0.0)
        scaled = (chip_sum(q, z) + from_left + from_right) * gain_ref[...]
        x_now = x_ref[0, piece_of(q), :].astype(F32)
        inv = lax.rsqrt(jnp.mean(x_now * x_now, axis=-1, keepdims=True) + EPSILON)
        dots = jnp.mean(scaled * x_now, axis=-1, keepdims=True)
        gloc[piece_of(q), :] = (
            cot_ref[0, piece_of(q), :].astype(F32) + inv * scaled - x_now * (inv**3 * dots)
        ).astype(BF16)
        shift_copy(q).start()
        return 0

    lax.fori_loop(0, cuts, finish, 0)

    def gain_wait(k, _):
        gain_copy(k, lax.rem(me + k, n)).wait_recv()
        gain_copy(k, me).wait_send()
        return 0

    lax.fori_loop(1, n, gain_wait, 0)
    ggain_out[...] = jnp.sum(gparts[...], axis=0)

    def ag_drain(b, _):
        for a in range(2):
            ag_each(a, b, lambda copy: copy.wait_send())
        sib_copy(b).wait_send()
        return 0

    lax.fori_loop(0, chips, ag_drain, 0)

    def line_drain(i, _):
        q, b = i // chips, i % chips

        @pl.when(b != z)
        def _():
            line_copy(q, b, b, me).wait_send()

        return 0

    lax.fori_loop(0, cuts * chips, line_drain, 0)
    store_wo.wait()
    store_wv.wait()

    def shift_wait(q, _):
        shift_copy(q).wait()
        return 0

    lax.fori_loop(0, cuts, shift_wait, 0)


def hand_on(splits, *refs):
    count = len(splits)
    sems = refs[2 * count]
    copies = []
    for source, target, parts in zip(refs[:count], refs[count : 2 * count], splits):
        height = source.shape[0] // parts
        for i in range(parts):
            cut = pl.ds(i * height, height)
            copies.append(
                pltpu.make_async_copy(source.at[cut], target.at[cut], sems.at[len(copies)])
            )
    for copy in copies:
        copy.start()
    for copy in copies:
        copy.wait()


def on_device(n, sections, x_in, grad_out, gain, w_val, w_out, filt, tail, micro_index):
    _, rows, width = x_in.shape
    channels = w_val.shape[1]
    chips = n // 2
    tokens = rows * n
    cuts = rows // 16
    vmem = pl.BlockSpec(memory_space=pltpu.VMEM)
    hbm = pl.BlockSpec(memory_space=pl.ANY)
    dma = pltpu.SemaphoreType.DMA
    shapes = (
        jax.ShapeDtypeStruct((rows, width), BF16),
        jax.ShapeDtypeStruct((channels, width), BF16),
        jax.ShapeDtypeStruct((channels, width), BF16),
        jax.ShapeDtypeStruct((TAPS, 1, channels), F32),
        jax.ShapeDtypeStruct(tail.shape, F32),
        jax.ShapeDtypeStruct(gain.shape, F32),
    )
    results = pl.pallas_call(
        functools.partial(kernel, n, sections, 512),
        out_shape=shapes,
        in_specs=[vmem, vmem, vmem, hbm, hbm, vmem, vmem, pl.BlockSpec(memory_space=pltpu.SMEM)],
        out_specs=(hbm, hbm, hbm, vmem, vmem, vmem),
        scratch_shapes=[
            pltpu.VMEM((tokens, width), BF16),
            pltpu.VMEM((tokens, width), BF16),
            pltpu.VMEM((channels, width), BF16),
            pltpu.VMEM((channels, width), BF16),
            pltpu.VMEM((tokens + 16, channels), F32),
            pltpu.VMEM((tokens + 8, channels), F32),
            pltpu.VMEM((tokens, channels), BF16),
            pltpu.VMEM((tokens, channels), BF16),
            pltpu.VMEM((channels, tokens), BF16),
            pltpu.VMEM((channels, tokens), BF16),
            pltpu.VMEM((channels, width), BF16),
            pltpu.VMEM((channels, width), BF16),
            pltpu.VMEM((rows, width), BF16),
            pltpu.VMEM((tokens, width), BF16),
            pltpu.VMEM((chips, rows, width), BF16),
            pltpu.VMEM((chips + 1, rows, width), BF16),
            pltpu.VMEM((chips, rows, width), BF16),
            pltpu.VMEM((n, 1, width), F32),
            pltpu.VMEM((1, width), F32),
            dma((3, 2, n)),
            dma((2, n)),
            dma((chips,)),
            dma((chips,)),
            dma((cuts, chips)),
            dma((cuts, chips + 1)),
            dma((n,)),
            dma((n,)),
            dma((3,)),
            dma((2,)),
            dma((cuts,)),
            dma((cuts,)),
        ],
        compiler_params=pltpu.CompilerParams(
            collective_id=0, has_side_effects=True, vmem_limit_bytes=60 * 2**20
        ),
    )(x_in, grad_out, gain, w_val, w_out, filt.transpose(1, 0, 2), tail, micro_index)
    splits = (1, 4, 4, 1, 1, 1)
    grad_in, grad_wv, grad_wo, grad_filter, grad_tail, grad_gain = pl.pallas_call(
        functools.partial(hand_on, splits),
        out_shape=shapes,
        in_specs=[hbm] * len(shapes),
        out_specs=(hbm,) * len(shapes),
        scratch_shapes=[dma((sum(splits),))],
        compiler_params=pltpu.CompilerParams(vmem_limit_bytes=60 * 2**20),
    )(*results)
    return (
        grad_in[None],
        grad_wv[None],
        grad_wo[None],
        grad_filter.transpose(1, 0, 2),
        grad_tail,
        grad_gain,
    )


def solution(mesh):
    placed = (
        P("section", "tensor", None),
        P("section", "tensor", None),
        P("section", None),
        P("section", "tensor", None),
        P("section", "tensor", None),
        P("section", None, "tensor"),
        P("section", None, "tensor"),
        P("section"),
    )
    return jax.shard_map(
        functools.partial(on_device, mesh.shape["tensor"], mesh.shape["section"]),
        mesh=mesh,
        in_specs=placed,
        out_specs=(
            P("section", "tensor", None),
            P("section", "tensor", None),
            P("section", "tensor", None),
            P("section", None, "tensor"),
            P("section", None, "tensor"),
            P("section", None),
        ),
        check_vma=False,
    )
```

```python
import functools

import jax
import jax.numpy as jnp
from jax import lax
from jax.experimental import pallas as pl
from jax.experimental.pallas import tpu as pltpu
from jax.sharding import PartitionSpec as P

TAPS = 3
EPSILON = 1e-06
MESH = pl.DeviceIdType.MESH
F32 = jnp.float32
BF16 = jnp.bfloat16


def dot_nt(left, right):
    return lax.dot_general(left, right, (((1,), (1,)), ((), ())), preferred_element_type=F32)


def dot_nn(left, right):
    return lax.dot_general(left, right, (((1,), (0,)), ((), ())), preferred_element_type=F32)


def kernel(
    n, sections, col_tile,
    x_ref, cot_ref, gain_ref, wv_hbm, wo_hbm, filt_ref, tail_ref, micro_ref,
    gin_out, gwv_out, gwo_out, gfilt_out, gtail_out, ggain_out,
    nrm, got, wv, wo, vals, gg, gat, gv, gat_t, gv_t, gwo, gwv, gloc, part, sib, inc, outg, gparts, own,
    ag_send, ag_recv, sib_send, sib_recv, line_send, line_recv,
    gain_send, gain_recv, load_sem, store_sem, shift_send, shift_recv,
):
    chips = n // 2
    rows = x_ref.shape[1]
    width = x_ref.shape[2]
    tokens = rows * n
    channels = wv.shape[0]
    height = 16
    cuts = rows // height
    hop = 2
    last = chips - 1
    me = lax.axis_index("tensor")
    z = me // 2
    c = me % 2
    other = z * 2 + (1 - c)
    sec = lax.axis_index("section")
    sec_prev = lax.rem(sec + sections - 1, sections)
    sec_next = lax.rem(sec + 1, sections)

    def rows_of(d):
        return pl.ds(pl.multiple_of(d * rows, rows), rows)

    def piece_of(q):
        return pl.ds(pl.multiple_of(q * height, height), height)

    load_cot = pltpu.make_async_copy(cot_ref.at[0], got.at[rows_of(me)], load_sem.at[0])
    load_wv = pltpu.make_async_copy(wv_hbm.at[0], wv, load_sem.at[1])
    load_wo = pltpu.make_async_copy(wo_hbm.at[0], wo, load_sem.at[2])
    load_cot.start()
    load_wo.start()
    load_wv.start()

    barrier = pltpu.get_barrier_semaphore()

    def greet(k, _):
        pl.semaphore_signal(
            barrier, inc=1, device_id={"tensor": lax.rem(me + k, n)}, device_id_type=MESH
        )
        return 0

    lax.fori_loop(1, n, greet, 0)
    pl.semaphore_signal(barrier, inc=1, device_id={"section": sec_prev}, device_id_type=MESH)
    pl.semaphore_signal(barrier, inc=1, device_id={"section": sec_next}, device_id_type=MESH)

    x_float = x_ref[0].astype(F32)
    inv_rms = lax.rsqrt(jnp.mean(x_float * x_float, axis=-1, keepdims=True) + EPSILON)
    nrm[rows_of(me), :] = (x_float * inv_rms * gain_ref[...]).astype(BF16)

    has_tail = (micro_ref[0] > 0).astype(F32)
    vals[0:8, :] = jnp.zeros((8, channels), F32)
    vals[6:8, :] = tail_ref[0].astype(F32) * has_tail
    vals[tokens + 8 : tokens + 16, :] = jnp.zeros((8, channels), F32)
    gg[tokens : tokens + 8, :] = jnp.zeros((8, channels), F32)
    gfilt_out[...] = jnp.zeros_like(gfilt_out)
    pl.semaphore_wait(barrier, n + 1)

    gathered = (got, nrm)

    def ag_copy(a, d, way, target):
        buf = gathered[a]
        return pltpu.make_async_remote_copy(
            src_ref=buf.at[rows_of(d)],
            dst_ref=buf.at[rows_of(d)],
            send_sem=ag_send.at[way, a, d],
            recv_sem=ag_recv.at[a, d],
            device_id={"tensor": target},
            device_id_type=MESH,
        )

    def ag_each(a, b, act):
        d = 2 * b + c

        @pl.when((b <= z) & (z < last))
        def _():
            act(ag_copy(a, d, 0, me + 2))

        @pl.when((b >= z) & (z > 0))
        def _():
            act(ag_copy(a, d, 1, me - 2))

        act(ag_copy(a, d, 2, other))

    def start(copy):
        copy.start()

    load_cot.wait()
    ag_each(0, z, start)
    ag_each(1, z, start)
    load_wo.wait()
    load_wv.wait()

    def project(a, b):
        ag_copy(a, 2 * b + (1 - c), 2, other).wait_recv()
        first = pl.multiple_of(b * 2 * rows, 2 * rows)
        pair = pl.ds(first, 2 * rows)
        if a == 0:
            gg[pair, :] = dot_nt(got[pair, :], wo[...])
        else:
            vals[pl.ds(pl.multiple_of(first + 8, 8), 2 * rows), :] = (
                dot_nt(nrm[pair, :], wv[...]).astype(BF16).astype(F32)
            )

    def project_at(a, s):
        @pl.when(z - s >= 0)
        def _():
            project(a, z - s)

        @pl.when((z + s < chips) & (s > 0))
        def _():
            project(a, z + s)

    def sib_copy(b):
        return pltpu.make_async_remote_copy(
            src_ref=part.at[rows_of(2 * b + (1 - c))],
            dst_ref=sib.at[b],
            send_sem=sib_send.at[b],
            recv_sem=sib_recv.at[b],
            device_id={"tensor": other},
            device_id_type=MESH,
        )

    def share(d, _):
        first = pl.multiple_of(d * rows, rows)

        def strip(i, _):
            cs = pl.ds(pl.multiple_of(i * 128, 128), 128)
            window = vals[pl.ds(first, rows + 16), cs]
            f = [filt_ref[k, :, cs] for k in range(TAPS)]
            v = window[8:]
            v1 = pltpu.roll(window, 1, 0)[8:]
            v2 = pltpu.roll(window, 2, 0)[8:]
            conv = f[0] * v + f[1] * v1 + f[2] * v2
            sig = jax.nn.sigmoid(conv)
            gat[rows_of(d), cs] = (conv * sig)[:rows].astype(BF16)
            gc = gg[pl.ds(first, rows + 8), cs] * sig * (1.0 + conv * (1.0 - sig))
            gc1 = pltpu.roll(gc, rows + 7, 0)[:rows]
            gc2 = pltpu.roll(gc, rows + 6, 0)[:rows]
            here = gc[:rows]
            for k, shifted in enumerate((v, v1, v2)):
                gfilt_out[k, :, cs] += jnp.sum(here * shifted[:rows], axis=0, keepdims=True)
            gv[rows_of(d), cs] = (f[0] * here + f[1] * gc1 + f[2] * gc2).astype(BF16)

            @pl.when(d == 0)
            def _():
                gtail_out[0, 0:1, cs] = f[2] * gc[0:1] * has_tail
                gtail_out[0, 1:2, cs] = (f[1] * gc[0:1] + f[2] * gc[1:2]) * has_tail

            return 0

        lax.fori_loop(0, channels // 128, strip, 0)

        def tile(j, _):
            cols = pl.ds(pl.multiple_of(j * col_tile, col_tile), col_tile)
            part[rows_of(d), cols] = dot_nn(gv[rows_of(d), :], wv[:, cols]).astype(BF16)
            return 0

        lax.fori_loop(0, width // col_tile, tile, 0)

        @pl.when(d % 2 != c)
        def _():
            sib_copy(d // 2).start()

        return 0

    def low_end(s):
        lo = z - s
        return jnp.where(lo > 0, 2 * lo + 1, 0)

    def high_end(s):
        hi = z + s
        return jnp.where(hi < last, 2 * hi + 1, n)

    def line_copy(q, b, slot, target):
        return pltpu.make_async_remote_copy(
            src_ref=outg.at[b, piece_of(q)],
            dst_ref=inc.at[slot, piece_of(q)],
            send_sem=line_send.at[q, b],
            recv_sem=line_recv.at[q, slot],
            device_id={"tensor": target},
            device_id_type=MESH,
        )

    def chip_sum(q, b):
        mine = pl.ds(pl.multiple_of((2 * b + c) * rows + q * height, height), height)
        return part[mine, :].astype(F32) + sib[b, piece_of(q), :].astype(F32)

    def forward(q, b, slot, target, upstream):
        @pl.when(q == 0)
        def _():
            sib_copy(b).wait_recv()

        @pl.when(upstream)
        def _():
            line_copy(q, b, b, me).wait_recv()
            outg[b, piece_of(q), :] = (
                chip_sum(q, b) + inc[b, piece_of(q), :].astype(F32)
            ).astype(BF16)

        @pl.when(jnp.logical_not(upstream))
        def _():
            outg[b, piece_of(q), :] = chip_sum(q, b).astype(BF16)

        line_copy(q, b, slot, target).start()

    def order(i, late):
        return jnp.where((late == 1) & (i >= last - 1), 2 * last - 1 - i, i)

    def right_at(t):
        u = t - hop * z
        b = order(u // cuts, c)

        @pl.when((u >= cuts) & (u < cuts * chips) & (b > z))
        def _():
            forward(u % cuts, b, jnp.where(b == z + 1, chips, b), me + 2, z > 0)

    def left_at(t):
        u = t - hop * (last - z)
        b = last - order(u // cuts, 1 - c)

        @pl.when((u >= cuts) & (u < cuts * chips) & (b < z))
        def _():
            forward(u % cuts, b, b, me - 2, z < last)

    def windows(s):
        def turn(q, _):
            right_at((s - c) * cuts + q)
            left_at((s - (1 - c)) * cuts + q)
            return 0

        lax.fori_loop(0, cuts, turn, 0)

    def shares(s, low, high):
        lax.fori_loop(low_end(s), low, share, 0)
        lax.fori_loop(high, high_end(s), share, 0)

    def gain_copy(k, d):
        return pltpu.make_async_remote_copy(
            src_ref=gparts.at[d],
            dst_ref=gparts.at[d],
            send_sem=gain_send.at[k],
            recv_sem=gain_recv.at[d],
            device_id={"tensor": lax.rem(me + k, n)},
            device_id_type=MESH,
        )

    store_wo = pltpu.make_async_copy(gwo, gwo_out, store_sem.at[0])
    store_wv = pltpu.make_async_copy(gwv, gwv_out, store_sem.at[1])

    def gain_part():
        def turned(i, _):
            cs = pl.ds(pl.multiple_of(i * 128, 128), 128)
            gat_t[cs, :] = gat[:, cs].astype(F32).T.astype(BF16)
            gv_t[cs, :] = gv[:, cs].astype(F32).T.astype(BF16)
            return 0

        lax.fori_loop(0, channels // 128, turned, 0)

        def tile(j, _):
            cols = pl.ds(pl.multiple_of(j * col_tile, col_tile), col_tile)
            grad = dot_nn(gv_t[...], nrm[:, cols])
            gwv[:, cols] = grad.astype(BF16)
            own[:, cols] = (
                jnp.sum(grad * wv[:, cols].astype(F32), axis=0, keepdims=True) / gain_ref[:, cols]
            )
            return 0

        lax.fori_loop(0, width // col_tile, tile, 0)
        store_wv.start()
        gparts[me] = own[...]

        def send(k, _):
            gain_copy(k, me).start()
            return 0

        lax.fori_loop(1, n, send, 0)

        def out_tile(j, _):
            cols = pl.ds(pl.multiple_of(j * col_tile, col_tile), col_tile)
            gwo[:, cols] = dot_nn(gat_t[...], got[:, cols]).astype(BF16)
            return 0

        lax.fori_loop(0, width // col_tile, out_tile, 0)
        store_wo.start()

    def process(s, low, high):
        project_at(1, s)
        shares(s, low, high)
        windows(s)

    inner = (z > 0) & (z < last)
    project_at(0, 0)
    process(0, 2 * z + 1, 2 * z + 1)

    def ag_step(s, _):
        for a in range(2):

            @pl.when(z - s >= 0)
            def _():
                ag_copy(a, 2 * (z - s) + c, 0, me).wait_recv()
                ag_each(a, z - s, start)

            @pl.when(z + s < chips)
            def _():
                ag_copy(a, 2 * (z + s) + c, 1, me).wait_recv()
                ag_each(a, z + s, start)

            if a == 0:
                project_at(0, s)

        process(s, low_end(s - 1), high_end(s - 1))

        @pl.when((s == last - 1) & inner)
        def _():
            gain_part()

        return 0

    lax.fori_loop(1, chips, ag_step, 0)

    def rest(t, _):
        right_at(t + (1 - c) * cuts)
        left_at(t + c * cuts)
        return 0

    lax.fori_loop(cuts * last, cuts * chips + hop * chips, rest, 0)

    @pl.when(jnp.logical_not(inner))
    def _():
        gain_part()

    def shift_copy(q):
        return pltpu.make_async_remote_copy(
            src_ref=gloc.at[piece_of(q)],
            dst_ref=gin_out.at[piece_of(q)],
            send_sem=shift_send.at[q],
            recv_sem=shift_recv.at[q],
            device_id={"section": sec_prev},
            device_id_type=MESH,
        )

    sib_copy(z).wait_recv()

    def finish(q, _):
        @pl.when(z > 0)
        def _():
            line_copy(q, z, chips, me).wait_recv()

        @pl.when(z < last)
        def _():
            line_copy(q, z, z, me).wait_recv()

        from_left = jnp.where(z > 0, inc[chips, piece_of(q), :].astype(F32), 0.0)
        from_right = jnp.where(z < last, inc[z, piece_of(q), :].astype(F32), 0.0)
        scaled = (chip_sum(q, z) + from_left + from_right) * gain_ref[...]
        x_now = x_ref[0, piece_of(q), :].astype(F32)
        inv = lax.rsqrt(jnp.mean(x_now * x_now, axis=-1, keepdims=True) + EPSILON)
        dots = jnp.mean(scaled * x_now, axis=-1, keepdims=True)
        gloc[piece_of(q), :] = (
            cot_ref[0, piece_of(q), :].astype(F32) + inv * scaled - x_now * (inv**3 * dots)
        ).astype(BF16)
        shift_copy(q).start()
        return 0

    lax.fori_loop(0, cuts, finish, 0)

    def gain_wait(k, _):
        gain_copy(k, lax.rem(me + k, n)).wait_recv()
        gain_copy(k, me).wait_send()
        return 0

    lax.fori_loop(1, n, gain_wait, 0)
    ggain_out[...] = jnp.sum(gparts[...], axis=0)

    def ag_drain(b, _):
        for a in range(2):
            ag_each(a, b, lambda copy: copy.wait_send())
        sib_copy(b).wait_send()
        return 0

    lax.fori_loop(0, chips, ag_drain, 0)

    def line_drain(i, _):
        q, b = i // chips, i % chips

        @pl.when(b != z)
        def _():
            line_copy(q, b, b, me).wait_send()

        return 0

    lax.fori_loop(0, cuts * chips, line_drain, 0)
    store_wo.wait()
    store_wv.wait()

    def shift_wait(q, _):
        shift_copy(q).wait()
        return 0

    lax.fori_loop(0, cuts, shift_wait, 0)


def hand_on(splits, *refs):
    count = len(splits)
    staged = refs[2 * count : 3 * count]
    sem_in, sem_out = refs[3 * count :]
    reads, writes = [], []
    for source, stage, target, parts in zip(refs[:count], staged, refs[count : 2 * count], splits):
        height = source.shape[0] // parts
        for i in range(parts):
            cut = pl.ds(i * height, height)
            at = len(reads)
            reads.append(pltpu.make_async_copy(source.at[cut], stage.at[cut], sem_in.at[at]))
            writes.append(pltpu.make_async_copy(stage.at[cut], target.at[cut], sem_out.at[at]))
    for read in reads:
        read.start()
    for read, write in zip(reads, writes):
        read.wait()
        write.start()
    for write in writes:
        write.wait()


def on_device(n, sections, x_in, grad_out, gain, w_val, w_out, filt, tail, micro_index):
    _, rows, width = x_in.shape
    channels = w_val.shape[1]
    chips = n // 2
    tokens = rows * n
    cuts = rows // 16
    vmem = pl.BlockSpec(memory_space=pltpu.VMEM)
    hbm = pl.BlockSpec(memory_space=pl.ANY)
    dma = pltpu.SemaphoreType.DMA
    shapes = (
        jax.ShapeDtypeStruct((rows, width), BF16),
        jax.ShapeDtypeStruct((channels, width), BF16),
        jax.ShapeDtypeStruct((channels, width), BF16),
        jax.ShapeDtypeStruct((TAPS, 1, channels), F32),
        jax.ShapeDtypeStruct(tail.shape, F32),
        jax.ShapeDtypeStruct(gain.shape, F32),
    )
    results = pl.pallas_call(
        functools.partial(kernel, n, sections, 512),
        out_shape=shapes,
        in_specs=[vmem, vmem, vmem, hbm, hbm, vmem, vmem, pl.BlockSpec(memory_space=pltpu.SMEM)],
        out_specs=(hbm, hbm, hbm, vmem, vmem, vmem),
        scratch_shapes=[
            pltpu.VMEM((tokens, width), BF16),
            pltpu.VMEM((tokens, width), BF16),
            pltpu.VMEM((channels, width), BF16),
            pltpu.VMEM((channels, width), BF16),
            pltpu.VMEM((tokens + 16, channels), F32),
            pltpu.VMEM((tokens + 8, channels), F32),
            pltpu.VMEM((tokens, channels), BF16),
            pltpu.VMEM((tokens, channels), BF16),
            pltpu.VMEM((channels, tokens), BF16),
            pltpu.VMEM((channels, tokens), BF16),
            pltpu.VMEM((channels, width), BF16),
            pltpu.VMEM((channels, width), BF16),
            pltpu.VMEM((rows, width), BF16),
            pltpu.VMEM((tokens, width), BF16),
            pltpu.VMEM((chips, rows, width), BF16),
            pltpu.VMEM((chips + 1, rows, width), BF16),
            pltpu.VMEM((chips, rows, width), BF16),
            pltpu.VMEM((n, 1, width), F32),
            pltpu.VMEM((1, width), F32),
            dma((3, 2, n)),
            dma((2, n)),
            dma((chips,)),
            dma((chips,)),
            dma((cuts, chips)),
            dma((cuts, chips + 1)),
            dma((n,)),
            dma((n,)),
            dma((3,)),
            dma((2,)),
            dma((cuts,)),
            dma((cuts,)),
        ],
        compiler_params=pltpu.CompilerParams(
            collective_id=0, has_side_effects=True, vmem_limit_bytes=60 * 2**20
        ),
    )(x_in, grad_out, gain, w_val, w_out, filt.transpose(1, 0, 2), tail, micro_index)
    splits = (1, 8, 8, 1, 1, 1)
    grad_in, grad_wv, grad_wo, grad_filter, grad_tail, grad_gain = pl.pallas_call(
        functools.partial(hand_on, splits),
        out_shape=shapes,
        in_specs=[hbm] * len(shapes),
        out_specs=(hbm,) * len(shapes),
        scratch_shapes=[pltpu.VMEM(shape.shape, shape.dtype) for shape in shapes]
        + [dma((sum(splits),)), dma((sum(splits),))],
        compiler_params=pltpu.CompilerParams(vmem_limit_bytes=60 * 2**20),
    )(*results)
    return (
        grad_in[None],
        grad_wv[None],
        grad_wo[None],
        grad_filter.transpose(1, 0, 2),
        grad_tail,
        grad_gain,
    )


def solution(mesh):
    placed = (
        P("section", "tensor", None),
        P("section", "tensor", None),
        P("section", None),
        P("section", "tensor", None),
        P("section", "tensor", None),
        P("section", None, "tensor"),
        P("section", None, "tensor"),
        P("section"),
    )
    return jax.shard_map(
        functools.partial(on_device, mesh.shape["tensor"], mesh.shape["section"]),
        mesh=mesh,
        in_specs=placed,
        out_specs=(
            P("section", "tensor", None),
            P("section", "tensor", None),
            P("section", "tensor", None),
            P("section", None, "tensor"),
            P("section", None, "tensor"),
            P("section", None),
        ),
        check_vma=False,
    )
```

```python
import functools

import jax
import jax.numpy as jnp
from jax import lax
from jax.experimental import pallas as pl
from jax.experimental.pallas import tpu as pltpu
from jax.sharding import PartitionSpec as P

TAPS = 3
EPSILON = 1e-06
MESH = pl.DeviceIdType.MESH
F32 = jnp.float32
BF16 = jnp.bfloat16


def dot_nt(left, right):
    return lax.dot_general(left, right, (((1,), (1,)), ((), ())), preferred_element_type=F32)


def dot_nn(left, right):
    return lax.dot_general(left, right, (((1,), (0,)), ((), ())), preferred_element_type=F32)


def kernel(
    n, sections, col_tile,
    x_ref, cot_ref, gain_ref, wv_hbm, wo_hbm, filt_ref, tail_ref, micro_ref,
    gin_out, gwv, gwo, gfilt_out, gtail_out, ggain_out,
    nrm, got, wv, wo, vals, gg, gat, gv, gat_t, gv_t, gloc, part, sib, inc, outg, gparts, own,
    ag_send, ag_recv, sib_send, sib_recv, line_send, line_recv,
    gain_send, gain_recv, load_sem, shift_send, shift_recv,
):
    chips = n // 2
    rows = x_ref.shape[1]
    width = x_ref.shape[2]
    tokens = rows * n
    channels = wv.shape[0]
    height = 16
    cuts = rows // height
    hop = 2
    last = chips - 1
    me = lax.axis_index("tensor")
    z = me // 2
    c = me % 2
    other = z * 2 + (1 - c)
    sec = lax.axis_index("section")
    sec_prev = lax.rem(sec + sections - 1, sections)
    sec_next = lax.rem(sec + 1, sections)

    def rows_of(d):
        return pl.ds(pl.multiple_of(d * rows, rows), rows)

    def piece_of(q):
        return pl.ds(pl.multiple_of(q * height, height), height)

    load_cot = pltpu.make_async_copy(cot_ref.at[0], got.at[rows_of(me)], load_sem.at[0])
    load_wv = pltpu.make_async_copy(wv_hbm.at[0], wv, load_sem.at[1])
    load_wo = pltpu.make_async_copy(wo_hbm.at[0], wo, load_sem.at[2])
    load_cot.start()
    load_wo.start()
    load_wv.start()

    barrier = pltpu.get_barrier_semaphore()

    def greet(k, _):
        pl.semaphore_signal(
            barrier, inc=1, device_id={"tensor": lax.rem(me + k, n)}, device_id_type=MESH
        )
        return 0

    lax.fori_loop(1, n, greet, 0)
    pl.semaphore_signal(barrier, inc=1, device_id={"section": sec_prev}, device_id_type=MESH)
    pl.semaphore_signal(barrier, inc=1, device_id={"section": sec_next}, device_id_type=MESH)

    x_float = x_ref[0].astype(F32)
    inv_rms = lax.rsqrt(jnp.mean(x_float * x_float, axis=-1, keepdims=True) + EPSILON)
    nrm[rows_of(me), :] = (x_float * inv_rms * gain_ref[...]).astype(BF16)

    has_tail = (micro_ref[0] > 0).astype(F32)
    vals[0:8, :] = jnp.zeros((8, channels), F32)
    vals[6:8, :] = tail_ref[0].astype(F32) * has_tail
    vals[tokens + 8 : tokens + 16, :] = jnp.zeros((8, channels), F32)
    gg[tokens : tokens + 8, :] = jnp.zeros((8, channels), F32)
    gfilt_out[...] = jnp.zeros_like(gfilt_out)
    pl.semaphore_wait(barrier, n + 1)

    gathered = (got, nrm)

    def ag_copy(a, d, way, target):
        buf = gathered[a]
        return pltpu.make_async_remote_copy(
            src_ref=buf.at[rows_of(d)],
            dst_ref=buf.at[rows_of(d)],
            send_sem=ag_send.at[way, a, d],
            recv_sem=ag_recv.at[a, d],
            device_id={"tensor": target},
            device_id_type=MESH,
        )

    def ag_each(a, b, act):
        d = 2 * b + c

        @pl.when((b <= z) & (z < last))
        def _():
            act(ag_copy(a, d, 0, me + 2))

        @pl.when((b >= z) & (z > 0))
        def _():
            act(ag_copy(a, d, 1, me - 2))

        act(ag_copy(a, d, 2, other))

    def start(copy):
        copy.start()

    load_cot.wait()
    ag_each(0, z, start)
    ag_each(1, z, start)
    load_wo.wait()
    load_wv.wait()

    def project(a, b):
        ag_copy(a, 2 * b + (1 - c), 2, other).wait_recv()
        first = pl.multiple_of(b * 2 * rows, 2 * rows)
        pair = pl.ds(first, 2 * rows)
        if a == 0:
            gg[pair, :] = dot_nt(got[pair, :], wo[...])
        else:
            vals[pl.ds(pl.multiple_of(first + 8, 8), 2 * rows), :] = (
                dot_nt(nrm[pair, :], wv[...]).astype(BF16).astype(F32)
            )

    def project_at(a, s):
        @pl.when(z - s >= 0)
        def _():
            project(a, z - s)

        @pl.when((z + s < chips) & (s > 0))
        def _():
            project(a, z + s)

    def sib_copy(b):
        return pltpu.make_async_remote_copy(
            src_ref=part.at[rows_of(2 * b + (1 - c))],
            dst_ref=sib.at[b],
            send_sem=sib_send.at[b],
            recv_sem=sib_recv.at[b],
            device_id={"tensor": other},
            device_id_type=MESH,
        )

    def share(d, _):
        first = pl.multiple_of(d * rows, rows)

        def strip(i, _):
            cs = pl.ds(pl.multiple_of(i * 128, 128), 128)
            window = vals[pl.ds(first, rows + 16), cs]
            f = [filt_ref[k, :, cs] for k in range(TAPS)]
            v = window[8:]
            v1 = pltpu.roll(window, 1, 0)[8:]
            v2 = pltpu.roll(window, 2, 0)[8:]
            conv = f[0] * v + f[1] * v1 + f[2] * v2
            sig = jax.nn.sigmoid(conv)
            gat[rows_of(d), cs] = (conv * sig)[:rows].astype(BF16)
            gc = gg[pl.ds(first, rows + 8), cs] * sig * (1.0 + conv * (1.0 - sig))
            gc1 = pltpu.roll(gc, rows + 7, 0)[:rows]
            gc2 = pltpu.roll(gc, rows + 6, 0)[:rows]
            here = gc[:rows]
            for k, shifted in enumerate((v, v1, v2)):
                gfilt_out[k, :, cs] += jnp.sum(here * shifted[:rows], axis=0, keepdims=True)
            gv[rows_of(d), cs] = (f[0] * here + f[1] * gc1 + f[2] * gc2).astype(BF16)

            @pl.when(d == 0)
            def _():
                gtail_out[0, 0:1, cs] = f[2] * gc[0:1] * has_tail
                gtail_out[0, 1:2, cs] = (f[1] * gc[0:1] + f[2] * gc[1:2]) * has_tail

            return 0

        lax.fori_loop(0, channels // 128, strip, 0)

        def tile(j, _):
            cols = pl.ds(pl.multiple_of(j * col_tile, col_tile), col_tile)
            part[rows_of(d), cols] = dot_nn(gv[rows_of(d), :], wv[:, cols]).astype(BF16)
            return 0

        lax.fori_loop(0, width // col_tile, tile, 0)

        @pl.when(d % 2 != c)
        def _():
            sib_copy(d // 2).start()

        return 0

    def low_end(s):
        lo = z - s
        return jnp.where(lo > 0, 2 * lo + 1, 0)

    def high_end(s):
        hi = z + s
        return jnp.where(hi < last, 2 * hi + 1, n)

    def line_copy(q, b, slot, target):
        return pltpu.make_async_remote_copy(
            src_ref=outg.at[b, piece_of(q)],
            dst_ref=inc.at[slot, piece_of(q)],
            send_sem=line_send.at[q, b],
            recv_sem=line_recv.at[q, slot],
            device_id={"tensor": target},
            device_id_type=MESH,
        )

    def chip_sum(q, b):
        mine = pl.ds(pl.multiple_of((2 * b + c) * rows + q * height, height), height)
        return part[mine, :].astype(F32) + sib[b, piece_of(q), :].astype(F32)

    def forward(q, b, slot, target, upstream):
        @pl.when(q == 0)
        def _():
            sib_copy(b).wait_recv()

        @pl.when(upstream)
        def _():
            line_copy(q, b, b, me).wait_recv()
            outg[b, piece_of(q), :] = (
                chip_sum(q, b) + inc[b, piece_of(q), :].astype(F32)
            ).astype(BF16)

        @pl.when(jnp.logical_not(upstream))
        def _():
            outg[b, piece_of(q), :] = chip_sum(q, b).astype(BF16)

        line_copy(q, b, slot, target).start()

    def order(i, late):
        return jnp.where((late == 1) & (i >= last - 1), 2 * last - 1 - i, i)

    def right_at(t):
        u = t - hop * z
        b = order(u // cuts, c)

        @pl.when((u >= cuts) & (u < cuts * chips) & (b > z))
        def _():
            forward(u % cuts, b, jnp.where(b == z + 1, chips, b), me + 2, z > 0)

    def left_at(t):
        u = t - hop * (last - z)
        b = last - order(u // cuts, 1 - c)

        @pl.when((u >= cuts) & (u < cuts * chips) & (b < z))
        def _():
            forward(u % cuts, b, b, me - 2, z < last)

    def windows(s):
        def turn(q, _):
            right_at((s - c) * cuts + q)
            left_at((s - (1 - c)) * cuts + q)
            return 0

        lax.fori_loop(0, cuts, turn, 0)

    def shares_and_sums(s, low, high):
        below = low - low_end(s)
        above = high_end(s) - high
        late_below = jnp.where((s == last) & (below > 0), 1, 0)
        late_above = jnp.where((s == last) & (above > 0), 1, 0)
        first = below - late_below

        def outer_share(k, _):
            return share(jnp.where(k < first, low_end(s) + k, high_end(s) - 1 - (k - first)), 0)

        lax.fori_loop(0, first + above - late_above, outer_share, 0)
        windows(s)

        def inner_share(k, _):
            return share(jnp.where(k < late_below, low - 1, high), 0)

        lax.fori_loop(0, late_below + late_above, inner_share, 0)

    def gain_copy(k, d):
        return pltpu.make_async_remote_copy(
            src_ref=gparts.at[d],
            dst_ref=gparts.at[d],
            send_sem=gain_send.at[k],
            recv_sem=gain_recv.at[d],
            device_id={"tensor": lax.rem(me + k, n)},
            device_id_type=MESH,
        )


    def gain_part():
        def turned(i, _):
            cs = pl.ds(pl.multiple_of(i * 128, 128), 128)
            gat_t[cs, :] = gat[:, cs].astype(F32).T.astype(BF16)
            gv_t[cs, :] = gv[:, cs].astype(F32).T.astype(BF16)
            return 0

        lax.fori_loop(0, channels // 128, turned, 0)

        def tile(j, _):
            cols = pl.ds(pl.multiple_of(j * col_tile, col_tile), col_tile)
            grad = dot_nn(gv_t[...], nrm[:, cols])
            gwv[:, cols] = grad.astype(BF16)
            own[:, cols] = (
                jnp.sum(grad * wv[:, cols].astype(F32), axis=0, keepdims=True) / gain_ref[:, cols]
            )
            return 0

        lax.fori_loop(0, width // col_tile, tile, 0)
        gparts[me] = own[...]

        def send(k, _):
            gain_copy(k, me).start()
            return 0

        lax.fori_loop(1, n, send, 0)

        def out_tile(j, _):
            cols = pl.ds(pl.multiple_of(j * col_tile, col_tile), col_tile)
            gwo[:, cols] = dot_nn(gat_t[...], got[:, cols]).astype(BF16)
            return 0

        lax.fori_loop(0, width // col_tile, out_tile, 0)

    def process(s, low, high):
        project_at(1, s)
        shares_and_sums(s, low, high)

    inner = (z > 0) & (z < last)
    project_at(0, 0)
    process(0, 2 * z + 1, 2 * z + 1)

    def ag_step(s, _):
        for a in range(2):

            @pl.when(z - s >= 0)
            def _():
                ag_copy(a, 2 * (z - s) + c, 0, me).wait_recv()
                ag_each(a, z - s, start)

            @pl.when(z + s < chips)
            def _():
                ag_copy(a, 2 * (z + s) + c, 1, me).wait_recv()
                ag_each(a, z + s, start)

            if a == 0:
                project_at(0, s)

        process(s, low_end(s - 1), high_end(s - 1))

        @pl.when((s == last - 1) & inner)
        def _():
            gain_part()

        return 0

    lax.fori_loop(1, chips, ag_step, 0)

    def rest(t, _):
        right_at(t + (1 - c) * cuts)
        left_at(t + c * cuts)
        return 0

    lax.fori_loop(cuts * last, cuts * chips + hop * chips, rest, 0)

    @pl.when(jnp.logical_not(inner))
    def _():
        gain_part()

    def shift_copy(q):
        return pltpu.make_async_remote_copy(
            src_ref=gloc.at[piece_of(q)],
            dst_ref=gin_out.at[piece_of(q)],
            send_sem=shift_send.at[q],
            recv_sem=shift_recv.at[q],
            device_id={"section": sec_prev},
            device_id_type=MESH,
        )

    sib_copy(z).wait_recv()

    def finish(q, _):
        @pl.when(z > 0)
        def _():
            line_copy(q, z, chips, me).wait_recv()

        @pl.when(z < last)
        def _():
            line_copy(q, z, z, me).wait_recv()

        from_left = jnp.where(z > 0, inc[chips, piece_of(q), :].astype(F32), 0.0)
        from_right = jnp.where(z < last, inc[z, piece_of(q), :].astype(F32), 0.0)
        scaled = (chip_sum(q, z) + from_left + from_right) * gain_ref[...]
        x_now = x_ref[0, piece_of(q), :].astype(F32)
        inv = lax.rsqrt(jnp.mean(x_now * x_now, axis=-1, keepdims=True) + EPSILON)
        dots = jnp.mean(scaled * x_now, axis=-1, keepdims=True)
        gloc[piece_of(q), :] = (
            cot_ref[0, piece_of(q), :].astype(F32) + inv * scaled - x_now * (inv**3 * dots)
        ).astype(BF16)
        shift_copy(q).start()
        return 0

    lax.fori_loop(0, cuts, finish, 0)

    def gain_wait(k, _):
        gain_copy(k, lax.rem(me + k, n)).wait_recv()
        gain_copy(k, me).wait_send()
        return 0

    lax.fori_loop(1, n, gain_wait, 0)
    ggain_out[...] = jnp.sum(gparts[...], axis=0)

    def ag_drain(b, _):
        for a in range(2):
            ag_each(a, b, lambda copy: copy.wait_send())
        sib_copy(b).wait_send()
        return 0

    lax.fori_loop(0, chips, ag_drain, 0)

    def line_drain(i, _):
        q, b = i // chips, i % chips

        @pl.when(b != z)
        def _():
            line_copy(q, b, b, me).wait_send()

        return 0

    lax.fori_loop(0, cuts * chips, line_drain, 0)

    def shift_wait(q, _):
        shift_copy(q).wait()
        return 0

    lax.fori_loop(0, cuts, shift_wait, 0)


def hand_on(splits, *refs):
    count = len(splits)
    sems = refs[2 * count]
    copies = []
    for source, target, parts in zip(refs[:count], refs[count : 2 * count], splits):
        height = source.shape[0] // parts
        for i in range(parts):
            cut = pl.ds(i * height, height)
            copies.append(
                pltpu.make_async_copy(source.at[cut], target.at[cut], sems.at[len(copies)])
            )
    for copy in copies:
        copy.start()
    for copy in copies:
        copy.wait()


def on_device(n, sections, x_in, grad_out, gain, w_val, w_out, filt, tail, micro_index):
    _, rows, width = x_in.shape
    channels = w_val.shape[1]
    chips = n // 2
    tokens = rows * n
    cuts = rows // 16
    vmem = pl.BlockSpec(memory_space=pltpu.VMEM)
    hbm = pl.BlockSpec(memory_space=pl.ANY)
    dma = pltpu.SemaphoreType.DMA
    shapes = (
        jax.ShapeDtypeStruct((rows, width), BF16),
        jax.ShapeDtypeStruct((channels, width), BF16),
        jax.ShapeDtypeStruct((channels, width), BF16),
        jax.ShapeDtypeStruct((TAPS, 1, channels), F32),
        jax.ShapeDtypeStruct(tail.shape, F32),
        jax.ShapeDtypeStruct(gain.shape, F32),
    )
    results = pl.pallas_call(
        functools.partial(kernel, n, sections, 512),
        out_shape=shapes[:1] + tuple(pltpu.VMEM(shape.shape, shape.dtype) for shape in shapes[1:]),
        in_specs=[vmem, vmem, vmem, hbm, hbm, vmem, vmem, pl.BlockSpec(memory_space=pltpu.SMEM)],
        out_specs=(hbm, vmem, vmem, vmem, vmem, vmem),
        scratch_shapes=[
            pltpu.VMEM((tokens, width), BF16),
            pltpu.VMEM((tokens, width), BF16),
            pltpu.VMEM((channels, width), BF16),
            pltpu.VMEM((channels, width), BF16),
            pltpu.VMEM((tokens + 16, channels), F32),
            pltpu.VMEM((tokens + 8, channels), F32),
            pltpu.VMEM((tokens, channels), BF16),
            pltpu.VMEM((tokens, channels), BF16),
            pltpu.VMEM((channels, tokens), BF16),
            pltpu.VMEM((channels, tokens), BF16),
            pltpu.VMEM((rows, width), BF16),
            pltpu.VMEM((tokens, width), BF16),
            pltpu.VMEM((chips, rows, width), BF16),
            pltpu.VMEM((chips + 1, rows, width), BF16),
            pltpu.VMEM((chips, rows, width), BF16),
            pltpu.VMEM((n, 1, width), F32),
            pltpu.VMEM((1, width), F32),
            dma((3, 2, n)),
            dma((2, n)),
            dma((chips,)),
            dma((chips,)),
            dma((cuts, chips)),
            dma((cuts, chips + 1)),
            dma((n,)),
            dma((n,)),
            dma((3,)),
            dma((cuts,)),
            dma((cuts,)),
        ],
        compiler_params=pltpu.CompilerParams(
            collective_id=0, has_side_effects=True, vmem_limit_bytes=50 * 2**20
        ),
    )(x_in, grad_out, gain, w_val, w_out, filt.transpose(1, 0, 2), tail, micro_index)
    splits = (1, 8, 8, 1, 1, 1)
    grad_in, grad_wv, grad_wo, grad_filter, grad_tail, grad_gain = pl.pallas_call(
        functools.partial(hand_on, splits),
        out_shape=shapes,
        in_specs=[vmem] * len(shapes),
        out_specs=(hbm,) * len(shapes),
        scratch_shapes=[dma((sum(splits),))],
        compiler_params=pltpu.CompilerParams(vmem_limit_bytes=16 * 2**20),
    )(*results)
    return (
        grad_in[None],
        grad_wv[None],
        grad_wo[None],
        grad_filter.transpose(1, 0, 2),
        grad_tail,
        grad_gain,
    )


def solution(mesh):
    placed = (
        P("section", "tensor", None),
        P("section", "tensor", None),
        P("section", None),
        P("section", "tensor", None),
        P("section", "tensor", None),
        P("section", None, "tensor"),
        P("section", None, "tensor"),
        P("section"),
    )
    return jax.shard_map(
        functools.partial(on_device, mesh.shape["tensor"], mesh.shape["section"]),
        mesh=mesh,
        in_specs=placed,
        out_specs=(
            P("section", "tensor", None),
            P("section", "tensor", None),
            P("section", "tensor", None),
            P("section", None, "tensor"),
            P("section", None, "tensor"),
            P("section", None),
        ),
        check_vma=False,
    )
```

```python
import functools

import jax
import jax.numpy as jnp
from jax import lax
from jax.experimental import pallas as pl
from jax.experimental.pallas import tpu as pltpu
from jax.sharding import PartitionSpec as P

TAPS = 3
EPSILON = 1e-06
MESH = pl.DeviceIdType.MESH
F32 = jnp.float32
BF16 = jnp.bfloat16


def dot_nt(left, right):
    return lax.dot_general(left, right, (((1,), (1,)), ((), ())), preferred_element_type=F32)


def dot_nn(left, right):
    return lax.dot_general(left, right, (((1,), (0,)), ((), ())), preferred_element_type=F32)


def kernel(
    n, sections, col_tile,
    x_ref, cot_ref, gain_ref, wv_hbm, wo_hbm, filt_ref, tail_ref, micro_ref,
    gin_out, gwv, gwo, gfilt_out, gtail_out, ggain_out,
    nrm, got, wv, wo, vals, gg, gat, gv, gat_t, gv_t, gloc, part, sib, inc, outg, gparts, own,
    ag_send, ag_recv, sib_send, sib_recv, line_send, line_recv,
    gain_send, gain_recv, load_sem, shift_send, shift_recv,
):
    chips = n // 2
    rows = x_ref.shape[1]
    width = x_ref.shape[2]
    tokens = rows * n
    channels = wv.shape[0]
    height = 16
    cuts = rows // height
    hop = 2
    last = chips - 1
    me = lax.axis_index("tensor")
    z = me // 2
    c = me % 2
    other = z * 2 + (1 - c)
    sec = lax.axis_index("section")
    sec_prev = lax.rem(sec + sections - 1, sections)
    sec_next = lax.rem(sec + 1, sections)

    def rows_of(d):
        return pl.ds(pl.multiple_of(d * rows, rows), rows)

    def piece_of(q):
        return pl.ds(pl.multiple_of(q * height, height), height)

    load_cot = pltpu.make_async_copy(cot_ref.at[0], got.at[rows_of(me)], load_sem.at[0])
    load_wv = pltpu.make_async_copy(wv_hbm.at[0], wv, load_sem.at[1])
    load_wo = pltpu.make_async_copy(wo_hbm.at[0], wo, load_sem.at[2])
    load_cot.start()
    load_wo.start()
    load_wv.start()

    barrier = pltpu.get_barrier_semaphore()

    def greet(k, _):
        pl.semaphore_signal(
            barrier, inc=1, device_id={"tensor": lax.rem(me + k, n)}, device_id_type=MESH
        )
        return 0

    lax.fori_loop(1, n, greet, 0)
    pl.semaphore_signal(barrier, inc=1, device_id={"section": sec_prev}, device_id_type=MESH)
    pl.semaphore_signal(barrier, inc=1, device_id={"section": sec_next}, device_id_type=MESH)

    x_float = x_ref[0].astype(F32)
    inv_rms = lax.rsqrt(jnp.mean(x_float * x_float, axis=-1, keepdims=True) + EPSILON)
    nrm[rows_of(me), :] = (x_float * inv_rms * gain_ref[...]).astype(BF16)

    has_tail = (micro_ref[0] > 0).astype(F32)
    vals[0:8, :] = jnp.zeros((8, channels), F32)
    vals[6:8, :] = tail_ref[0].astype(F32) * has_tail
    vals[tokens + 8 : tokens + 16, :] = jnp.zeros((8, channels), F32)
    gg[tokens : tokens + 8, :] = jnp.zeros((8, channels), F32)
    gfilt_out[...] = jnp.zeros_like(gfilt_out)
    pl.semaphore_wait(barrier, n + 1)

    gathered = (got, nrm)

    def ag_copy(a, d, way, target):
        buf = gathered[a]
        return pltpu.make_async_remote_copy(
            src_ref=buf.at[rows_of(d)],
            dst_ref=buf.at[rows_of(d)],
            send_sem=ag_send.at[way, a, d],
            recv_sem=ag_recv.at[a, d],
            device_id={"tensor": target},
            device_id_type=MESH,
        )

    def ag_each(a, b, act):
        d = 2 * b + c

        @pl.when((b <= z) & (z < last))
        def _():
            act(ag_copy(a, d, 0, me + 2))

        @pl.when((b >= z) & (z > 0))
        def _():
            act(ag_copy(a, d, 1, me - 2))

        act(ag_copy(a, d, 2, other))

    def start(copy):
        copy.start()

    load_cot.wait()
    ag_each(0, z, start)
    ag_each(1, z, start)
    load_wo.wait()
    load_wv.wait()

    def project(a, b):
        ag_copy(a, 2 * b + (1 - c), 2, other).wait_recv()
        first = pl.multiple_of(b * 2 * rows, 2 * rows)
        pair = pl.ds(first, 2 * rows)
        if a == 0:
            gg[pair, :] = dot_nt(got[pair, :], wo[...])
        else:
            vals[pl.ds(pl.multiple_of(first + 8, 8), 2 * rows), :] = (
                dot_nt(nrm[pair, :], wv[...]).astype(BF16).astype(F32)
            )

    def project_at(a, s):
        @pl.when(z - s >= 0)
        def _():
            project(a, z - s)

        @pl.when((z + s < chips) & (s > 0))
        def _():
            project(a, z + s)

    def sib_copy(b):
        return pltpu.make_async_remote_copy(
            src_ref=part.at[rows_of(2 * b + (1 - c))],
            dst_ref=sib.at[b],
            send_sem=sib_send.at[b],
            recv_sem=sib_recv.at[b],
            device_id={"tensor": other},
            device_id_type=MESH,
        )

    def share(d, blocks):
        height = blocks * rows
        first = pl.multiple_of(d * rows, rows)
        span = pl.ds(first, height)

        def strip(i, _):
            cs = pl.ds(pl.multiple_of(i * 128, 128), 128)
            window = vals[pl.ds(first, height + 16), cs]
            f = [filt_ref[k, :, cs] for k in range(TAPS)]
            v = window[8:]
            v1 = pltpu.roll(window, 1, 0)[8:]
            v2 = pltpu.roll(window, 2, 0)[8:]
            conv = f[0] * v + f[1] * v1 + f[2] * v2
            sig = jax.nn.sigmoid(conv)
            gat[span, cs] = (conv * sig)[:height].astype(BF16)
            gc = gg[pl.ds(first, height + 8), cs] * sig * (1.0 + conv * (1.0 - sig))
            gc1 = pltpu.roll(gc, height + 7, 0)[:height]
            gc2 = pltpu.roll(gc, height + 6, 0)[:height]
            here = gc[:height]
            for k, shifted in enumerate((v, v1, v2)):
                gfilt_out[k, :, cs] += jnp.sum(here * shifted[:height], axis=0, keepdims=True)
            gv[span, cs] = (f[0] * here + f[1] * gc1 + f[2] * gc2).astype(BF16)

            @pl.when(d == 0)
            def _():
                gtail_out[0, 0:1, cs] = f[2] * gc[0:1] * has_tail
                gtail_out[0, 1:2, cs] = (f[1] * gc[0:1] + f[2] * gc[1:2]) * has_tail

            return 0

        lax.fori_loop(0, channels // 128, strip, 0)

        def tile(j, _):
            cols = pl.ds(pl.multiple_of(j * col_tile, col_tile), col_tile)
            part[span, cols] = dot_nn(gv[span, :], wv[:, cols]).astype(BF16)
            return 0

        lax.fori_loop(0, width // col_tile, tile, 0)

        given = jnp.where(d % 2 != c, d, d + 1)

        @pl.when(given < d + blocks)
        def _():
            sib_copy(given // 2).start()

    def low_end(s):
        lo = z - s
        return jnp.where(lo > 0, 2 * lo + 1, 0)

    def high_end(s):
        hi = z + s
        return jnp.where(hi < last, 2 * hi + 1, n)

    def line_copy(q, b, slot, target):
        return pltpu.make_async_remote_copy(
            src_ref=outg.at[b, piece_of(q)],
            dst_ref=inc.at[slot, piece_of(q)],
            send_sem=line_send.at[q, b],
            recv_sem=line_recv.at[q, slot],
            device_id={"tensor": target},
            device_id_type=MESH,
        )

    def chip_sum(q, b):
        mine = pl.ds(pl.multiple_of((2 * b + c) * rows + q * height, height), height)
        return part[mine, :].astype(F32) + sib[b, piece_of(q), :].astype(F32)

    def forward(q, b, slot, target, upstream):
        @pl.when(q == 0)
        def _():
            sib_copy(b).wait_recv()

        @pl.when(upstream)
        def _():
            line_copy(q, b, b, me).wait_recv()
            outg[b, piece_of(q), :] = (
                chip_sum(q, b) + inc[b, piece_of(q), :].astype(F32)
            ).astype(BF16)

        @pl.when(jnp.logical_not(upstream))
        def _():
            outg[b, piece_of(q), :] = chip_sum(q, b).astype(BF16)

        line_copy(q, b, slot, target).start()

    def order(i, late):
        return jnp.where((late == 1) & (i >= last - 1), 2 * last - 1 - i, i)

    def right_at(t):
        u = t - hop * z
        b = order(u // cuts, c)

        @pl.when((u >= cuts) & (u < cuts * chips) & (b > z))
        def _():
            forward(u % cuts, b, jnp.where(b == z + 1, chips, b), me + 2, z > 0)

    def left_at(t):
        u = t - hop * (last - z)
        b = last - order(u // cuts, 1 - c)

        @pl.when((u >= cuts) & (u < cuts * chips) & (b < z))
        def _():
            forward(u % cuts, b, b, me - 2, z < last)

    def windows(s):
        def turn(q, _):
            right_at((s - c) * cuts + q)
            left_at((s - (1 - c)) * cuts + q)
            return 0

        lax.fori_loop(0, cuts, turn, 0)

    def shares_and_sums(s, low, high):
        below = low - low_end(s)
        above = high_end(s) - high
        low_pairs, high_pairs = below // 2, above // 2
        odd_low, odd_high = below % 2, above % 2

        def pair_share(k, _):
            share(
                jnp.where(
                    k < low_pairs, low_end(s) + 2 * k, high_end(s) - 2 - 2 * (k - low_pairs)
                ),
                2,
            )
            return 0

        def odd_share(k, _):
            share(jnp.where(k < odd_low, low - 1, high), 1)
            return 0

        lax.fori_loop(0, low_pairs + high_pairs, pair_share, 0)
        lax.fori_loop(0, jnp.where(s < last, odd_low + odd_high, 0), odd_share, 0)
        windows(s)
        lax.fori_loop(0, jnp.where(s == last, odd_low + odd_high, 0), odd_share, 0)

    def gain_copy(k, d):
        return pltpu.make_async_remote_copy(
            src_ref=gparts.at[d],
            dst_ref=gparts.at[d],
            send_sem=gain_send.at[k],
            recv_sem=gain_recv.at[d],
            device_id={"tensor": lax.rem(me + k, n)},
            device_id_type=MESH,
        )


    def gain_part():
        def turned(i, _):
            cs = pl.ds(pl.multiple_of(i * 128, 128), 128)
            gat_t[cs, :] = gat[:, cs].astype(F32).T.astype(BF16)
            gv_t[cs, :] = gv[:, cs].astype(F32).T.astype(BF16)
            return 0

        lax.fori_loop(0, channels // 128, turned, 0)

        def tile(j, _):
            cols = pl.ds(pl.multiple_of(j * col_tile, col_tile), col_tile)
            grad = dot_nn(gv_t[...], nrm[:, cols])
            gwv[:, cols] = grad.astype(BF16)
            own[:, cols] = (
                jnp.sum(grad * wv[:, cols].astype(F32), axis=0, keepdims=True) / gain_ref[:, cols]
            )
            return 0

        lax.fori_loop(0, width // col_tile, tile, 0)
        gparts[me] = own[...]

        def send(k, _):
            gain_copy(k, me).start()
            return 0

        lax.fori_loop(1, n, send, 0)

        def out_tile(j, _):
            cols = pl.ds(pl.multiple_of(j * col_tile, col_tile), col_tile)
            gwo[:, cols] = dot_nn(gat_t[...], got[:, cols]).astype(BF16)
            return 0

        lax.fori_loop(0, width // col_tile, out_tile, 0)

    def process(s, low, high):
        project_at(1, s)
        shares_and_sums(s, low, high)

    inner = (z > 0) & (z < last)
    project_at(0, 0)
    process(0, 2 * z + 1, 2 * z + 1)

    def ag_step(s, _):
        for a in range(2):

            @pl.when(z - s >= 0)
            def _():
                ag_copy(a, 2 * (z - s) + c, 0, me).wait_recv()
                ag_each(a, z - s, start)

            @pl.when(z + s < chips)
            def _():
                ag_copy(a, 2 * (z + s) + c, 1, me).wait_recv()
                ag_each(a, z + s, start)

            if a == 0:
                project_at(0, s)

        process(s, low_end(s - 1), high_end(s - 1))

        @pl.when((s == last - 1) & inner)
        def _():
            gain_part()

        return 0

    lax.fori_loop(1, chips, ag_step, 0)

    def rest(t, _):
        right_at(t + (1 - c) * cuts)
        left_at(t + c * cuts)
        return 0

    lax.fori_loop(cuts * last, cuts * chips + hop * chips, rest, 0)

    @pl.when(jnp.logical_not(inner))
    def _():
        gain_part()

    def shift_copy(q):
        return pltpu.make_async_remote_copy(
            src_ref=gloc.at[piece_of(q)],
            dst_ref=gin_out.at[piece_of(q)],
            send_sem=shift_send.at[q],
            recv_sem=shift_recv.at[q],
            device_id={"section": sec_prev},
            device_id_type=MESH,
        )

    sib_copy(z).wait_recv()

    def finish(q, _):
        @pl.when(z > 0)
        def _():
            line_copy(q, z, chips, me).wait_recv()

        @pl.when(z < last)
        def _():
            line_copy(q, z, z, me).wait_recv()

        from_left = jnp.where(z > 0, inc[chips, piece_of(q), :].astype(F32), 0.0)
        from_right = jnp.where(z < last, inc[z, piece_of(q), :].astype(F32), 0.0)
        scaled = (chip_sum(q, z) + from_left + from_right) * gain_ref[...]
        x_now = x_ref[0, piece_of(q), :].astype(F32)
        inv = lax.rsqrt(jnp.mean(x_now * x_now, axis=-1, keepdims=True) + EPSILON)
        dots = jnp.mean(scaled * x_now, axis=-1, keepdims=True)
        gloc[piece_of(q), :] = (
            cot_ref[0, piece_of(q), :].astype(F32) + inv * scaled - x_now * (inv**3 * dots)
        ).astype(BF16)
        shift_copy(q).start()
        return 0

    lax.fori_loop(0, cuts, finish, 0)

    def gain_wait(k, _):
        gain_copy(k, lax.rem(me + k, n)).wait_recv()
        gain_copy(k, me).wait_send()
        return 0

    lax.fori_loop(1, n, gain_wait, 0)
    ggain_out[...] = jnp.sum(gparts[...], axis=0)

    def ag_drain(b, _):
        for a in range(2):
            ag_each(a, b, lambda copy: copy.wait_send())
        sib_copy(b).wait_send()
        return 0

    lax.fori_loop(0, chips, ag_drain, 0)

    def line_drain(i, _):
        q, b = i // chips, i % chips

        @pl.when(b != z)
        def _():
            line_copy(q, b, b, me).wait_send()

        return 0

    lax.fori_loop(0, cuts * chips, line_drain, 0)

    def shift_wait(q, _):
        shift_copy(q).wait()
        return 0

    lax.fori_loop(0, cuts, shift_wait, 0)


def hand_on(splits, *refs):
    count = len(splits)
    sems = refs[2 * count]
    copies = []
    for source, target, parts in zip(refs[:count], refs[count : 2 * count], splits):
        height = source.shape[0] // parts
        for i in range(parts):
            cut = pl.ds(i * height, height)
            copies.append(
                pltpu.make_async_copy(source.at[cut], target.at[cut], sems.at[len(copies)])
            )
    for copy in copies:
        copy.start()
    for copy in copies:
        copy.wait()


def on_device(n, sections, x_in, grad_out, gain, w_val, w_out, filt, tail, micro_index):
    _, rows, width = x_in.shape
    channels = w_val.shape[1]
    chips = n // 2
    tokens = rows * n
    cuts = rows // 16
    vmem = pl.BlockSpec(memory_space=pltpu.VMEM)
    hbm = pl.BlockSpec(memory_space=pl.ANY)
    dma = pltpu.SemaphoreType.DMA
    shapes = (
        jax.ShapeDtypeStruct((rows, width), BF16),
        jax.ShapeDtypeStruct((channels, width), BF16),
        jax.ShapeDtypeStruct((channels, width), BF16),
        jax.ShapeDtypeStruct((TAPS, 1, channels), F32),
        jax.ShapeDtypeStruct(tail.shape, F32),
        jax.ShapeDtypeStruct(gain.shape, F32),
    )
    results = pl.pallas_call(
        functools.partial(kernel, n, sections, 512),
        out_shape=tuple(pltpu.VMEM(shape.shape, shape.dtype) for shape in shapes),
        in_specs=[vmem, vmem, vmem, hbm, hbm, vmem, vmem, pl.BlockSpec(memory_space=pltpu.SMEM)],
        out_specs=(vmem,) * len(shapes),
        scratch_shapes=[
            pltpu.VMEM((tokens, width), BF16),
            pltpu.VMEM((tokens, width), BF16),
            pltpu.VMEM((channels, width), BF16),
            pltpu.VMEM((channels, width), BF16),
            pltpu.VMEM((tokens + 16, channels), F32),
            pltpu.VMEM((tokens + 8, channels), F32),
            pltpu.VMEM((tokens, channels), BF16),
            pltpu.VMEM((tokens, channels), BF16),
            pltpu.VMEM((channels, tokens), BF16),
            pltpu.VMEM((channels, tokens), BF16),
            pltpu.VMEM((rows, width), BF16),
            pltpu.VMEM((tokens, width), BF16),
            pltpu.VMEM((chips, rows, width), BF16),
            pltpu.VMEM((chips + 1, rows, width), BF16),
            pltpu.VMEM((chips, rows, width), BF16),
            pltpu.VMEM((n, 1, width), F32),
            pltpu.VMEM((1, width), F32),
            dma((3, 2, n)),
            dma((2, n)),
            dma((chips,)),
            dma((chips,)),
            dma((cuts, chips)),
            dma((cuts, chips + 1)),
            dma((n,)),
            dma((n,)),
            dma((3,)),
            dma((cuts,)),
            dma((cuts,)),
        ],
        compiler_params=pltpu.CompilerParams(
            collective_id=0, has_side_effects=True, vmem_limit_bytes=50 * 2**20
        ),
    )(x_in, grad_out, gain, w_val, w_out, filt.transpose(1, 0, 2), tail, micro_index)
    splits = (1, 8, 8, 1, 1, 1)
    grad_in, grad_wv, grad_wo, grad_filter, grad_tail, grad_gain = pl.pallas_call(
        functools.partial(hand_on, splits),
        out_shape=shapes,
        in_specs=[vmem] * len(shapes),
        out_specs=(hbm,) * len(shapes),
        scratch_shapes=[dma((sum(splits),))],
        compiler_params=pltpu.CompilerParams(vmem_limit_bytes=16 * 2**20),
    )(*results)
    return (
        grad_in[None],
        grad_wv[None],
        grad_wo[None],
        grad_filter.transpose(1, 0, 2),
        grad_tail,
        grad_gain,
    )


def solution(mesh):
    placed = (
        P("section", "tensor", None),
        P("section", "tensor", None),
        P("section", None),
        P("section", "tensor", None),
        P("section", "tensor", None),
        P("section", None, "tensor"),
        P("section", None, "tensor"),
        P("section"),
    )
    return jax.shard_map(
        functools.partial(on_device, mesh.shape["tensor"], mesh.shape["section"]),
        mesh=mesh,
        in_specs=placed,
        out_specs=(
            P("section", "tensor", None),
            P("section", "tensor", None),
            P("section", "tensor", None),
            P("section", None, "tensor"),
            P("section", None, "tensor"),
            P("section", None),
        ),
        check_vma=False,
    )
```
